32 devices in a mesh: dp: 8 (over z, x), mp: 4 (over y, core).
Axes of the slice: x: 2, y: 2, z: 4, core: 2. Of those that a mesh axis runs over, the one named last changes fastest.
Arguments:
- features: bfloat16 [8, 320, 128, 128], P('dp', 'mp'), may hold values from -6 to 6
- w_out: bfloat16 [320, 36], P('mp'), may hold values from -0.109375 to 0.109375
- noisy_latent: float32 [8, 4, 128, 128], P('dp', None, 'mp'), may hold values from -6 to 6
- timestep: int32 [8], P('dp'), may hold values from 100 to 699
- w_in: bfloat16 [9, 512, 4], replicated, may hold values from -1 to 1
- b_in: float32 [512], replicated, may hold values from -3 to 3
- w_mid: bfloat16 [9, 512, 512], replicated, may hold values from -0.09375 to 0.09375
- b_mid: float32 [512], replicated, may hold values from -3 to 3
- reward_head: float32 [512], replicated, may hold values from -6 to 6
Outputs:
- feature_grads: bfloat16 [8, 320, 128, 128], P('dp', 'mp')
- weight_grad: float32 [320, 36], P('mp')
The draws below stay inside these ranges and needn't reach their ends.
All inputs are finite; a program needn't handle non-finite values.
Results may differ from the reference program's by a relative error of at most 0.012.
Values may be sent and summed in bfloat16 or wider, within the bound.
No kernel may reach another device: no remote copies, remote signals or barrier semaphores. Data moves between devices by JAX's collectives and lax.ppermute only.
A program may use at most 192 MiB of HBM per device.

```python
import jax
import jax.numpy as jnp
from jax import lax

CU = 320
CD = 512
LAT = 4
CROP = 128
W = 128
IMAGES = 8


def with_ends(drawn, stream_key, least, top_value):
    shape = drawn.shape
    spot = [jax.random.randint(jax.random.fold_in(stream_key, axis), (), 0, shape[axis]) for axis in range(len(shape))]
    drawn = drawn.at[tuple(spot)].set(least)
    longest = shape.index(max(shape))
    spot[longest] = (spot[longest] + 1) % shape[longest]
    return drawn.at[tuple(spot)].set(top_value)


def shard_levels(rng, shape, shards, least, largest):
    def one(dim, blocks):
        steps = jax.random.uniform(jax.random.fold_in(jax.random.fold_in(rng, 6), dim), (blocks,), jnp.float32, least / len(shards), largest / len(shards))
        return jnp.repeat(jnp.exp(steps), shape[dim] // blocks).reshape((-1,) + (1,) * (len(shape) - dim - 1))

    gain = one(*shards[0])
    for cut in shards[1:]:
        gain = gain * one(*cut)
    return gain


def noise(rng, shape, spread, reach, split=(), kind=jnp.bfloat16):
    factor_of = shard_levels(rng, shape, split, -0.22, 0.18) if split else 1.0
    array = jax.random.normal(rng, shape, jnp.float32) * spread * factor_of
    return jnp.minimum(jnp.maximum(array, -reach), reach).astype(kind)


def setup_inputs(seed: int = 0) -> dict:
    key_of = jax.random.split(jax.random.key(seed), 10)
    return {
        "features": noise(key_of[0], (IMAGES, CU, CROP, W), 1.0, 6.0, ((0, 8), (1, 4))),
        "w_out": noise(key_of[1], (CU, 9 * LAT), (9 * CU) ** -0.5, 0.109375, ((0, 4),)),
        "noisy_latent": noise(key_of[2], (IMAGES, LAT, CROP, W), 1.0, 6.0, ((0, 8), (2, 4)), jnp.float32),
        "timestep": with_ends(jax.random.randint(key_of[3], (IMAGES,), 100, 700), jax.random.fold_in(key_of[3], 1), 100, 699).astype(jnp.int32),
        "w_in": noise(key_of[4], (9, CD, LAT), (9 * LAT) ** -0.5, 1.0),
        "b_in": noise(key_of[5], (CD,), 0.5, 3.0, (), jnp.float32),
        "w_mid": noise(key_of[6], (9, CD, CD), (9 * CD) ** -0.5, 0.09375),
        "b_mid": noise(key_of[7], (CD,), 0.5, 3.0, (), jnp.float32),
        "reward_head": noise(key_of[8], (CD,), 1.0, 6.0, (), jnp.float32),
    }


def noise_levels(timestep):
    betas = jnp.linspace(0.00085 ** 0.5, 0.012 ** 0.5, 1000, dtype=jnp.float32) ** 2
    table = jnp.cumprod(1.0 - betas).astype(jnp.float32)
    hits = jnp.arange(1000, dtype=jnp.int32)[None, :] == timestep[:, None]
    return lax.optimization_barrier(jnp.sum(jnp.where(hits, table[None, :], jnp.float32(0.0)), axis=1))

def pad_both(source):
    return jnp.pad(source, ((0, 0), (1, 1), (1, 1)))

def slope(value):
    sig = jax.nn.sigmoid(value)
    return sig * (1.0 + value * (1.0 - sig))

def conv_taps(padded, kernel, out_rows, out_cols):
    summed = jnp.zeros((kernel.shape[1], out_rows * out_cols), jnp.float32)
    for tap in range(9):
        tap_row, tap_col = (tap // 3, tap % 3)
        window = padded[:, tap_row:tap_row + out_rows, tap_col:tap_col + out_cols].reshape(padded.shape[0], -1)
        summed = summed + jnp.dot(kernel[tap], window, preferred_element_type=jnp.float32)
    return summed.reshape(kernel.shape[1], out_rows, out_cols)

def conv_back(padded, kernel, out_rows, out_cols):
    summed = jnp.zeros((kernel.shape[2], out_rows * out_cols), jnp.float32)
    for tap in range(9):
        tap_row, tap_col = (tap // 3, tap % 3)
        window = padded[:, 2 - tap_row:2 - tap_row + out_rows, 2 - tap_col:2 - tap_col + out_cols].reshape(padded.shape[0], -1)
        summed = summed + jnp.dot(kernel[tap].T, window, preferred_element_type=jnp.float32)
    return summed.reshape(kernel.shape[2], out_rows, out_cols)

def weight_taps(padded, noise_grad, out_rows, out_cols):
    flat = noise_grad.reshape(noise_grad.shape[0], -1)
    parts = []
    for tap in range(9):
        tap_row, tap_col = (tap // 3, tap % 3)
        window = padded[:, tap_row:tap_row + out_rows, tap_col:tap_col + out_cols].reshape(padded.shape[0], -1)
        parts.append(jnp.dot(window, flat.T, preferred_element_type=jnp.float32))
    return jnp.concatenate(parts, axis=1)

def reference(features, w_out, noisy_latent, timestep, w_in, b_in, w_mid, b_mid, reward_head):
    channels = features.shape[1]
    lat_chans = noisy_latent.shape[1]
    crop_rows, col_count = (features.shape[2], features.shape[3])
    eps_kernel = jnp.transpose(w_out.reshape(channels, 9, lat_chans), (1, 2, 0))
    noise_level = noise_levels(timestep)
    root_a = jnp.sqrt(noise_level)
    root_b = jnp.sqrt(1.0 - noise_level)

    def one_image(packed):
        feats, noisy, coef_a, coef_b = packed
        feat_pad = pad_both(feats)
        eps = conv_taps(feat_pad, eps_kernel, crop_rows, col_count)
        latent = ((noisy - coef_b * eps) / coef_a).astype(jnp.bfloat16)
        hidden_pre = conv_taps(pad_both(latent), w_in, crop_rows, col_count) + b_in[:, None, None]
        hidden_act = jax.nn.silu(hidden_pre).astype(jnp.bfloat16)
        mixed_pre = conv_taps(pad_both(hidden_act), w_mid, crop_rows, col_count) + b_mid[:, None, None]
        mixed_grad = (reward_head[:, None, None] * slope(mixed_pre)).astype(jnp.bfloat16)
        act_grad = conv_back(pad_both(mixed_grad), w_mid, crop_rows, col_count)
        hidden_grad = (act_grad * slope(hidden_pre)).astype(jnp.bfloat16)
        latent_grad = conv_back(pad_both(hidden_grad), w_in, crop_rows, col_count)
        noise_grad = (-(coef_b / coef_a) * latent_grad).astype(jnp.bfloat16)
        feat_grads = conv_back(pad_both(noise_grad), eps_kernel, crop_rows, col_count).astype(jnp.bfloat16)
        return (feat_grads, weight_taps(feat_pad, noise_grad, crop_rows, col_count))
    feature_grads, weight_parts = lax.map(one_image, (features, noisy_latent, root_a, root_b))
    weight_grad = lax.optimization_barrier(jnp.sum(weight_parts, axis=0)) / (crop_rows * col_count)
    return (feature_grads, weight_grad)
```

```python
import functools

import jax
import jax.numpy as jnp
import numpy as np
from jax import lax
from jax.experimental import pallas as pl
from jax.experimental.pallas import tpu as pltpu
from jax.sharding import PartitionSpec as P

BLOCK = 16
HALO = 4
TILE = 4
PT_A = 0.5**0.5
PT_B = 2.0**0.5
STEPS = 1000
F32 = jnp.float32
BF16 = jnp.bfloat16


def dot(lhs, rhs, lhs_dim, rhs_dim):
    return lax.dot_general(
        lhs, rhs, (((lhs_dim,), (rhs_dim,)), ((), ())), preferred_element_type=F32
    )


def schedule_table():
    betas = np.linspace(0.00085**0.5, 0.012**0.5, STEPS, dtype=np.float32) ** 2
    table = np.cumprod(np.float32(1.0) - betas, dtype=np.float32)
    return np.pad(table, (0, 1024 - STEPS)).reshape(8, 128)


def roots(table_ref, step):
    rows = lax.broadcasted_iota(jnp.int32, (8, 128), 0)
    cols = lax.broadcasted_iota(jnp.int32, (8, 128), 1)
    hit = jnp.where(rows * 128 + cols == step, table_ref[...], 0.0)
    level = jnp.sum(jnp.sum(hit, axis=1, keepdims=True), axis=0, keepdims=True)
    return jnp.sqrt(level), jnp.sqrt(1.0 - level)


def band_tables(channels, lat):
    wide = BLOCK + 2
    tall = 3 * wide * lat
    picks = np.zeros((3, tall, 9 * lat), np.float32)
    for tap_row in range(3):
        for tap_col in range(3):
            for row in range(wide):
                for chan in range(lat):
                    spot = (tap_col * wide + row) * lat + chan
                    picks[tap_row, spot, (3 * tap_row + tap_col) * lat + chan] = 1.0
    spread = np.kron(np.eye(channels, dtype=np.float32), np.ones((1, BLOCK), np.float32))
    out_row = np.tile(np.repeat(np.arange(wide, dtype=np.int32), lat), 3)
    in_row = np.tile(np.arange(BLOCK, dtype=np.int32), channels)
    return picks, spread, out_row, in_row


def column_tables(cols):
    tiles = cols // TILE
    place = np.arange(cols)
    source = TILE * (place % tiles) + place // tiles
    gather = np.zeros((3, cols, cols), np.float32)
    scatter = np.zeros((3, cols, cols), np.float32)
    for tap_col in range(3):
        for spot in range(cols):
            taken = source[spot] + tap_col - 1
            if 0 <= taken < cols:
                gather[tap_col, taken, spot] = 1.0
                scatter[tap_col, spot, taken] = 1.0
    return gather, scatter.reshape(3 * cols, cols)


def eps_kernel(
    step_ref, me_ref, feat_ref, wout_ref, noisy_ref, table_ref, picks_ref, spread_ref,
    out_row_ref, in_row_ref, *refs, parts, rows, height, lat
):
    outs = refs[:parts]
    acc_ref, sum_ref, own_ref = refs[parts:]
    channels, cols = feat_ref.shape[0], feat_ref.shape[2]
    group = (BLOCK + 2) * lat
    gap = in_row_ref[...] - out_row_ref[...]
    band = jnp.zeros(gap.shape, F32)
    for tap_row in range(3):
        taps = dot(picks_ref[tap_row], wout_ref[...], 1, 1).astype(BF16)
        band = jnp.where(gap == tap_row - 2, dot(taps, spread_ref[...], 1, 0), band)
    band = band.astype(BF16)
    acc_ref[...] = jnp.zeros(acc_ref.shape, F32)
    for block in range(height // BLOCK):
        feats = feat_ref[:, block * BLOCK : (block + 1) * BLOCK, :]
        part = dot(band, feats.reshape(channels * BLOCK, cols), 1, 0)
        low = block * BLOCK * lat
        for tap_col in range(3):
            acc_ref[tap_col, low : low + group, :] += part[tap_col * group : (tap_col + 1) * group]
    spot = lax.broadcasted_iota(jnp.int32, (height * lat, cols), 1)
    inner = slice(lat, lat + height * lat)
    left = jnp.where(spot == 0, 0.0, pltpu.roll(acc_ref[0, inner, :], 1, 1))
    right = jnp.where(spot == cols - 1, 0.0, pltpu.roll(acc_ref[2, inner, :], cols - 1, 1))
    eps = left + acc_ref[1, inner, :] + right
    _, root_b = roots(table_ref, step_ref[0])
    edge = HALO * lat
    sum_ref[0:edge, :] = jnp.zeros((edge, cols), F32)
    sum_ref[edge + height * lat :, :] = jnp.zeros((edge, cols), F32)
    sum_ref[edge : edge + height * lat, :] = -root_b * eps
    for chan in range(lat):
        own_ref[pl.ds(chan, rows, stride=lat), :] = noisy_ref[0, chan]
    me = me_ref[0]
    low = pl.multiple_of(me * (rows * lat) + edge, 16)
    sum_ref[pl.ds(low, rows * lat), :] += own_ref[...]
    for part in range(parts):
        low = pl.multiple_of((me ^ part) * (rows * lat), 16)
        outs[part][...] = sum_ref[pl.ds(low, (rows + 2 * HALO) * lat), :].astype(BF16)


def prep_kernel(
    wmid_ref, wout_ref, picks_ref, spread_ref, out_row_ref, in_row_ref, planes_ref, band_ref
):
    for tap_row in range(3):
        first = wmid_ref[3 * tap_row].astype(F32)
        mid = wmid_ref[3 * tap_row + 1].astype(F32)
        last = wmid_ref[3 * tap_row + 2].astype(F32)
        even = (-2.0 / 3.0) * first + (-1.0 / 3.0) * last
        odd = (-2.0 / 3.0 * PT_A) * mid
        planes_ref[0, tap_row] = (even + odd).astype(BF16)
        planes_ref[1, tap_row] = (even - odd).astype(BF16)
        even = (1.0 / 6.0) * first + (1.0 / 3.0) * last
        odd = (1.0 / 6.0 * PT_B) * mid
        planes_ref[2, tap_row] = (even + odd).astype(BF16)
        planes_ref[3, tap_row] = (even - odd).astype(BF16)
    gap = in_row_ref[...] - out_row_ref[...]
    tall = dot(spread_ref[...], wout_ref[...], 0, 0).astype(BF16)
    band = jnp.zeros(gap.shape, F32)
    for tap_row in range(3):
        band = jnp.where(gap == tap_row - 2, dot(tall, picks_ref[tap_row], 1, 1), band)
    band_ref[...] = band.astype(BF16)


def to_planes(cells):
    tiles, chans = cells[0].shape
    none = jnp.zeros((1, chans), F32)
    d0 = jnp.concatenate([none, cells[3][: tiles - 1]], axis=0)
    d1, d2, d3, d4 = cells
    d5 = jnp.concatenate([cells[0][1:], none], axis=0)
    s1, s3 = PT_A * d1, PT_A * d3
    even_a, odd_a = d4 - 2.0 * d2, s3 - 2.0 * s1
    even_b, odd_b = d4 - 0.5 * d2, 2.0 * s3 - s1
    return (
        (d0 + d4) - 2.5 * d2,
        even_a + odd_a,
        even_a - odd_a,
        even_b + odd_b,
        even_b - odd_b,
        (d1 + d5) - 2.5 * d3,
    )


def from_planes(m0, ap, an, bp, bn, m5):
    sum_a, dif_a, sum_b, dif_b = ap + an, PT_A * (ap - an), bp + bn, PT_B * (bp - bn)
    return (
        m0 + sum_a + sum_b,
        dif_a + dif_b,
        0.5 * sum_a + 2.0 * sum_b,
        0.5 * dif_a + 2.0 * dif_b + m5,
    )


def from_planes_back(m0, ap, an, bp, bn, m5):
    sum_a, dif_a, sum_b, dif_b = ap + an, PT_A * (ap - an), bp + bn, PT_B * (bp - bn)
    return (
        m0 - 2.0 * sum_a - 0.5 * sum_b,
        -(2.0 * dif_a + 0.5 * dif_b),
        -(sum_a + sum_b),
        m5 - (dif_a + dif_b),
    )


def chunk_of(rows):
    return max(size for size in range(1, 19) if rows % size == 0)


def decoder_kernel(
    step_ref, me_ref, *refs, parts, rows, lat, cols
):
    blocks = refs[:parts]
    (table_ref, gather_ref, scatter_ref, win_ref, bin_ref, wback_ref, wmid_ref, planes_ref,
     bmid_ref, head_ref, out_ref, lat_ref, v1_ref, v2_ref, slope_ref, m_ref, hg_ref, x_ref,
     q_ref, lg_ref) = refs[parts:]
    tiles = cols // TILE
    me = me_ref[0]
    root_a, root_b = roots(table_ref, step_ref[0])
    total = blocks[0][...].astype(F32)
    for block in blocks[1:]:
        total = total + block[...].astype(F32)
    latent = (total / root_a).astype(BF16)
    lat_rows = (rows + 2 * HALO) * lat
    for tap_col in range(3):
        lat_ref[tap_col, 0:lat_rows, :] = dot(latent, gather_ref[tap_col], 1, 0)
        lat_ref[tap_col, lat_rows:, :] = jnp.zeros((8, cols), F32)

    hidden_rows, mixed_rows, grad_rows = rows + 6, rows + 4, rows + 2

    def hidden_step(pair, carry):
        wins = []
        for tap_col in range(3):
            low = pl.multiple_of(pair * 8, 8)
            rows24 = lat_ref[tap_col, pl.ds(low, 24), :]
            wins.append(jnp.concatenate([rows24[0:16], rows24[4:20]], axis=1))
        window = jnp.concatenate(wins, axis=0).astype(BF16)
        pre = dot(window, win_ref[...], 0, 0) + bin_ref[...]
        sig = 0.5 + 0.5 * jnp.tanh(0.5 * pre)
        act = pre * sig
        low = pl.multiple_of(pair * (2 * cols), 2 * cols)
        slope_ref[pl.ds(low, 2 * cols), :] = sig + act * (1.0 - sig)
        for half in range(2):
            cells = [
                act[half * cols + part * tiles : half * cols + (part + 1) * tiles]
                for part in range(TILE)
            ]
            low = pl.multiple_of((2 * pair + half) * tiles, tiles)
            for plane, value in enumerate(to_planes(cells)):
                v1_ref[plane, pl.ds(low, tiles), :] = value.astype(BF16)
        return carry

    lax.fori_loop(0, hidden_rows // 2, hidden_step, 0)

    def clear(ref, count, total_rows, width):
        @pl.when(me == 0)
        def _():
            for plane in range(ref.shape[0]):
                ref[plane, 0 : count * width, :] = jnp.zeros((count * width, ref.shape[2]), BF16)

        @pl.when(me == parts - 1)
        def _():
            for plane in range(ref.shape[0]):
                ref[plane, (total_rows - count) * width : total_rows * width, :] = jnp.zeros(
                    (count * width, ref.shape[2]), BF16
                )

    clear(v1_ref, 3, hidden_rows, tiles)

    chunk = chunk_of(mixed_rows)

    def mixed_chunk(index, carry):
        base = index * chunk
        for plane in range(6):
            value = None
            for tap_row in range(3):
                if plane == 0:
                    kern = wmid_ref[3 * tap_row]
                elif plane == 5:
                    kern = wmid_ref[3 * tap_row + 2]
                else:
                    kern = planes_ref[plane - 1, tap_row]
                low = pl.multiple_of((base + tap_row) * tiles, tiles)
                part = dot(v1_ref[plane, pl.ds(low, chunk * tiles), :], kern, 1, 1)
                value = part if value is None else value + part
            m_ref[plane, 0 : chunk * tiles, :] = value

        def mixed_step(row, inner):
            low = pl.multiple_of(row * tiles, tiles)
            cells = from_planes(*[m_ref[plane, pl.ds(low, tiles), :] for plane in range(6)])
            grads = []
            for cell in cells:
                pre = cell + bmid_ref[...]
                sig = 0.5 + 0.5 * jnp.tanh(0.5 * pre)
                grads.append(head_ref[...] * (sig * (1.0 + pre * (1.0 - sig))))
            low = pl.multiple_of((base + row) * tiles, tiles)
            for plane, value in enumerate(to_planes(grads)):
                v2_ref[plane, pl.ds(low, tiles), :] = value.astype(BF16)
            return inner

        lax.fori_loop(0, chunk, mixed_step, 0)
        return carry

    lax.fori_loop(0, mixed_rows // chunk, mixed_chunk, 0)
    clear(v2_ref, 2, mixed_rows, tiles)

    back = chunk_of(grad_rows)

    def grad_chunk(index, carry):
        base = index * back
        for plane in range(6):
            value = None
            for shift in range(3):
                tap_row = 2 - shift
                if plane == 0:
                    kern = wmid_ref[3 * tap_row + 2]
                elif plane == 5:
                    kern = wmid_ref[3 * tap_row]
                else:
                    kern = planes_ref[(plane - 1) ^ 2, tap_row]
                low = pl.multiple_of((base + shift) * tiles, tiles)
                part = dot(v2_ref[plane, pl.ds(low, back * tiles), :], kern, 1, 0)
                value = part if value is None else value + part
            m_ref[plane, 0 : back * tiles, :] = value

        def grad_step(row, inner):
            low = pl.multiple_of(row * tiles, tiles)
            cells = from_planes_back(*[m_ref[plane, pl.ds(low, tiles), :] for plane in range(6)])
            for part, cell in enumerate(cells):
                low = pl.multiple_of((base + row) * cols + part * tiles, tiles)
                slope_low = pl.multiple_of((base + row + 2) * cols + part * tiles, tiles)
                hg_ref[0, pl.ds(low, tiles), :] = (
                    cell * slope_ref[pl.ds(slope_low, tiles), :]
                ).astype(BF16)
            return inner

        lax.fori_loop(0, back, grad_step, 0)
        return carry

    lax.fori_loop(0, grad_rows // back, grad_chunk, 0)
    clear(hg_ref, 1, grad_rows, cols)

    taps = dot(wback_ref[...], hg_ref[0], 1, 1)
    for row in range(grad_rows):
        for tap_col in range(3):
            x_ref[16 * row : 16 * row + 16, tap_col * cols : (tap_col + 1) * cols] = taps[
                16 * tap_col : 16 * tap_col + 16, row * cols : (row + 1) * cols
            ]
    value = x_ref[...]
    high = value.astype(BF16)
    rest = (value - high.astype(F32)).astype(BF16)
    q_ref[...] = dot(high, scatter_ref[...], 1, 0) + dot(rest, scatter_ref[...], 1, 0)
    for row in range(rows):
        lg_ref[lat * row : lat * row + lat, :] = (
            q_ref[16 * (row + 2) : 16 * (row + 2) + lat, :]
            + q_ref[16 * (row + 1) + lat : 16 * (row + 1) + 2 * lat, :]
            + q_ref[16 * row + 2 * lat : 16 * row + 3 * lat, :]
        )
    out_ref[...] = (-(root_b / root_a) * lg_ref[...]).astype(BF16)


def fill_windows(noise_ref, win_ref, lat):
    tall, cols = noise_ref.shape
    noise = noise_ref[...].astype(F32)
    spot = lax.broadcasted_iota(jnp.int32, (tall, cols), 1)
    none = jnp.zeros((lat, cols), F32)
    moved = (
        jnp.where(spot == cols - 1, 0.0, pltpu.roll(noise, cols - 1, 1)),
        noise,
        jnp.where(spot == 0, 0.0, pltpu.roll(noise, 1, 1)),
    )
    for tap_col in range(3):
        win_ref[tap_col, 0:lat, :] = none
        win_ref[tap_col, lat : lat + tall, :] = moved[tap_col]
        win_ref[tap_col, lat + tall :, :] = none


def window_of(win_ref, block, lat):
    low = block * BLOCK * lat
    group = (BLOCK + 2) * lat
    return jnp.concatenate(
        [win_ref[tap_col, low : low + group, :] for tap_col in range(3)], axis=0
    ).astype(BF16)


def weight_kernel(
    feat_ref, noise_ref, picks_ref, out_row_ref, in_row_ref, out_ref, win_ref, *, lat
):
    channels, height, cols = feat_ref.shape
    fill_windows(noise_ref, win_ref, lat)
    total = None
    for block in range(height // BLOCK):
        feats = feat_ref[:, block * BLOCK : (block + 1) * BLOCK, :]
        part = dot(feats.reshape(channels * BLOCK, cols), window_of(win_ref, block, lat), 1, 1)
        total = part if total is None else total + part
    gap = in_row_ref[...] - out_row_ref[...]
    result = jnp.zeros(out_ref.shape, F32)
    for tap_row in range(3):
        kept = jnp.where(gap == tap_row - 2, total, 0.0)
        summed = jnp.sum(kept.reshape(channels, BLOCK, -1), axis=1)
        high = summed.astype(BF16)
        rest = summed - high.astype(F32)
        mid = rest.astype(BF16)
        low = (rest - mid.astype(F32)).astype(BF16)
        for piece in (high, mid, low):
            result = result + dot(piece, picks_ref[tap_row], 1, 0)
    out_ref[...] = result


def feature_kernel(band_ref, noise_ref, out_ref, win_ref, *, lat):
    channels, height, cols = out_ref.shape
    fill_windows(noise_ref, win_ref, lat)
    for block in range(height // BLOCK):
        value = dot(band_ref[...], window_of(win_ref, block, lat), 1, 0)
        out_ref[:, block * BLOCK : (block + 1) * BLOCK, :] = value.astype(BF16).reshape(
            channels, BLOCK, cols
        )


VMEM = pl.BlockSpec(memory_space=pltpu.VMEM)
SMEM = pl.BlockSpec(memory_space=pltpu.SMEM)
PARAMS = pltpu.CompilerParams(vmem_limit_bytes=60 * 2**20)


def call(kernel, scalars, operands, outs, scratch, name):
    return pl.pallas_call(
        kernel,
        in_specs=[SMEM] * len(scalars) + [VMEM] * len(operands),
        out_specs=jax.tree.map(lambda _: VMEM, outs),
        out_shape=outs,
        scratch_shapes=scratch,
        compiler_params=PARAMS,
        name=name,
    )(*scalars, *operands)


def body(features, w_out, noisy_latent, timestep, w_in, b_in, w_mid, b_mid, reward_head):
    _, channels, height, cols = features.shape
    lat, rows = noisy_latent.shape[1:3]
    chans = w_mid.shape[1]
    tiles = cols // TILE
    parts, images = lax.axis_size("mp"), lax.axis_size("dp")
    feats = features[0]
    me = lax.axis_index("mp").astype(jnp.int32).reshape(1)
    table = jnp.asarray(schedule_table())
    picks, spread, out_row, in_row = band_tables(channels, lat)
    picks, spread = jnp.asarray(picks, BF16), jnp.asarray(spread, BF16)
    gather, scatter = (jnp.asarray(part, BF16) for part in column_tables(cols))
    tall, deep = 3 * (BLOCK + 2) * lat, channels * BLOCK
    block_rows = (rows + 2 * HALO) * lat

    blocks = call(
        functools.partial(eps_kernel, parts=parts, rows=rows, height=height, lat=lat),
        (timestep, me),
        (feats, w_out, noisy_latent, table, picks, spread, out_row[:, None], in_row[None, :]),
        [jax.ShapeDtypeStruct((block_rows, cols), BF16) for _ in range(parts)],
        [
            pltpu.VMEM((3, (height + 2) * lat, cols), F32),
            pltpu.VMEM(((height + 2 * HALO) * lat, cols), F32),
            pltpu.VMEM((rows * lat, cols), F32),
        ],
        "eps_partial",
    )
    moved = [blocks[0]] + [
        lax.ppermute(blocks[part], "mp", [(i, i ^ part) for i in range(parts)])
        for part in range(1, parts)
    ]
    planes, band = call(
        prep_kernel,
        (),
        (w_mid, w_out, picks, spread, out_row[None, :], in_row[:, None]),
        [
            jax.ShapeDtypeStruct((4, 3, chans, chans), BF16),
            jax.ShapeDtypeStruct((deep, tall), BF16),
        ],
        [],
        "weight_planes",
    )
    taps = w_in.reshape(3, 3, chans, lat)
    win = jnp.pad(
        jnp.transpose(taps, (1, 0, 3, 2)).reshape(3, 3 * lat, chans), ((0, 0), (0, 16 - 3 * lat), (0, 0))
    ).reshape(48, chans)
    noise = call(
        functools.partial(decoder_kernel, parts=parts, rows=rows, lat=lat, cols=cols),
        (timestep, me),
        (*moved, table, gather, scatter, win, b_in[None, :], win, w_mid, planes, b_mid[None, :],
         reward_head[None, :]),
        jax.ShapeDtypeStruct((rows * lat, cols), BF16),
        [
            pltpu.VMEM((3, block_rows + 8, cols), F32),
            pltpu.VMEM((6, (rows + 6) * tiles, chans), BF16),
            pltpu.VMEM((6, (rows + 4) * tiles, chans), BF16),
            pltpu.VMEM(((rows + 6) * cols, chans), F32),
            pltpu.VMEM((6, max(chunk_of(rows + 4), chunk_of(rows + 2)) * tiles, chans), F32),
            pltpu.VMEM((1, (rows + 2) * cols, chans), BF16),
            pltpu.VMEM(((rows + 2) * 16, 3 * cols), F32),
            pltpu.VMEM(((rows + 2) * 16, cols), F32),
            pltpu.VMEM((rows * lat, cols), F32),
        ],
        "decoder",
    )
    full = lax.all_gather(noise, "mp", axis=0, tiled=True)
    weight_grad = call(
        functools.partial(weight_kernel, lat=lat),
        (),
        (feats, full, picks, out_row[None, :], in_row[:, None]),
        jax.ShapeDtypeStruct((channels, 9 * lat), F32),
        [pltpu.VMEM((3, (height + 2) * lat, cols), F32)],
        "weight_grad",
    )
    stage = 1
    while stage < images:
        weight_grad = weight_grad + lax.ppermute(
            weight_grad, "dp", [(i, i ^ stage) for i in range(images)]
        )
        stage *= 2
    feature_grads = call(
        functools.partial(feature_kernel, lat=lat),
        (),
        (band, full),
        jax.ShapeDtypeStruct((channels, height, cols), BF16),
        [pltpu.VMEM((3, (height + 2) * lat, cols), F32)],
        "feature_grads",
    )
    return feature_grads[None], weight_grad / (height * cols)


def solution(mesh):
    in_specs = (
        P("dp", "mp", None, None),
        P("mp", None),
        P("dp", None, "mp", None),
        P("dp"),
        P(),
        P(),
        P(),
        P(),
        P(),
    )
    out_specs = (P("dp", "mp", None, None), P("mp", None))
    return jax.shard_map(body, mesh=mesh, in_specs=in_specs, out_specs=out_specs, check_vma=False)
```

```python
import functools

import jax
import jax.numpy as jnp
import numpy as np
from jax import lax
from jax.experimental import pallas as pl
from jax.experimental.pallas import tpu as pltpu
from jax.sharding import PartitionSpec as P

BLOCK = 16
HALO = 4
TILE = 4
PT_A = 0.5**0.5
PT_B = 2.0**0.5
STEPS = 1000
CHUNK = 9
LANES = 256
QUOTA = 4.5
F32 = jnp.float32
BF16 = jnp.bfloat16


def dot(lhs, rhs, lhs_dim, rhs_dim):
    return lax.dot_general(
        lhs, rhs, (((lhs_dim,), (rhs_dim,)), ((), ())), preferred_element_type=F32
    )


def schedule_table():
    betas = np.linspace(0.00085**0.5, 0.012**0.5, STEPS, dtype=np.float32) ** 2
    table = np.cumprod(np.float32(1.0) - betas, dtype=np.float32)
    return np.pad(table, (0, 1024 - STEPS)).reshape(8, 128)


def roots(table_ref, step):
    rows = lax.broadcasted_iota(jnp.int32, (8, 128), 0)
    cols = lax.broadcasted_iota(jnp.int32, (8, 128), 1)
    hit = jnp.where(rows * 128 + cols == step, table_ref[...], 0.0)
    level = jnp.sum(jnp.sum(hit, axis=1, keepdims=True), axis=0, keepdims=True)
    return jnp.sqrt(level), jnp.sqrt(1.0 - level)


def band_tables(channels, lat):
    wide = BLOCK + 2
    tall = 3 * wide * lat
    picks = np.zeros((3, tall, 9 * lat), np.float32)
    for tap_row in range(3):
        for tap_col in range(3):
            for row in range(wide):
                for chan in range(lat):
                    spot = (tap_col * wide + row) * lat + chan
                    picks[tap_row, spot, (3 * tap_row + tap_col) * lat + chan] = 1.0
    spread = np.kron(np.eye(channels, dtype=np.float32), np.ones((1, BLOCK), np.float32))
    out_row = np.tile(np.repeat(np.arange(wide, dtype=np.int32), lat), 3)
    in_row = np.tile(np.arange(BLOCK, dtype=np.int32), channels)
    return picks, spread, out_row, in_row


def column_tables(cols):
    tiles = cols // TILE
    place = np.arange(cols)
    source = TILE * (place % tiles) + place // tiles
    gather = np.zeros((3, cols, cols), np.float32)
    scatter = np.zeros((3, cols, cols), np.float32)
    for tap_col in range(3):
        for spot in range(cols):
            taken = source[spot] + tap_col - 1
            if 0 <= taken < cols:
                gather[tap_col, taken, spot] = 1.0
                scatter[tap_col, spot, taken] = 1.0
    return gather, scatter.reshape(3 * cols, cols)


def eps_kernel(
    step_ref, me_ref, feat_ref, wout_ref, noisy_ref, table_ref, picks_ref, spread_ref,
    out_row_ref, in_row_ref, *refs, parts, rows, height, lat
):
    outs = refs[:parts]
    acc_ref, sum_ref, own_ref = refs[parts:]
    channels, cols = feat_ref.shape[0], feat_ref.shape[2]
    group = (BLOCK + 2) * lat
    gap = in_row_ref[...] - out_row_ref[...]
    band = jnp.zeros(gap.shape, F32)
    for tap_row in range(3):
        taps = dot(picks_ref[tap_row], wout_ref[...], 1, 1).astype(BF16)
        band = jnp.where(gap == tap_row - 2, dot(taps, spread_ref[...], 1, 0), band)
    band = band.astype(BF16)
    acc_ref[...] = jnp.zeros(acc_ref.shape, F32)
    for block in range(height // BLOCK):
        feats = feat_ref[:, block * BLOCK : (block + 1) * BLOCK, :]
        part = dot(band, feats.reshape(channels * BLOCK, cols), 1, 0)
        low = block * BLOCK * lat
        for tap_col in range(3):
            acc_ref[tap_col, low : low + group, :] += part[tap_col * group : (tap_col + 1) * group]
    spot = lax.broadcasted_iota(jnp.int32, (height * lat, cols), 1)
    inner = slice(lat, lat + height * lat)
    left = jnp.where(spot == 0, 0.0, pltpu.roll(acc_ref[0, inner, :], 1, 1))
    right = jnp.where(spot == cols - 1, 0.0, pltpu.roll(acc_ref[2, inner, :], cols - 1, 1))
    eps = left + acc_ref[1, inner, :] + right
    _, root_b = roots(table_ref, step_ref[0])
    edge = HALO * lat
    sum_ref[0:edge, :] = jnp.zeros((edge, cols), F32)
    sum_ref[edge + height * lat :, :] = jnp.zeros((edge, cols), F32)
    sum_ref[edge : edge + height * lat, :] = -root_b * eps
    for chan in range(lat):
        own_ref[pl.ds(chan, rows, stride=lat), :] = noisy_ref[0, chan]
    me = me_ref[0]
    low = pl.multiple_of(me * (rows * lat) + edge, 16)
    sum_ref[pl.ds(low, rows * lat), :] += own_ref[...]
    for part in range(parts):
        low = pl.multiple_of((me ^ part) * (rows * lat), 16)
        outs[part][...] = sum_ref[pl.ds(low, (rows + 2 * HALO) * lat), :].astype(BF16)


def prep_kernel(
    wmid_ref, wout_ref, picks_ref, spread_ref, out_row_ref, in_row_ref, planes_ref, band_ref
):
    first = wmid_ref[0].astype(F32)
    mid = wmid_ref[1].astype(F32)
    last = wmid_ref[2].astype(F32)
    even = (-2.0 / 3.0) * first + (-1.0 / 3.0) * last
    odd = (-2.0 / 3.0 * PT_A) * mid
    planes_ref[0, 0] = (even + odd).astype(BF16)
    planes_ref[1, 0] = (even - odd).astype(BF16)
    even = (1.0 / 6.0) * first + (1.0 / 3.0) * last
    odd = (1.0 / 6.0 * PT_B) * mid
    planes_ref[2, 0] = (even + odd).astype(BF16)
    planes_ref[3, 0] = (even - odd).astype(BF16)

    @pl.when((pl.program_id(0) == 0) & (pl.program_id(1) == 0))
    def _():
        gap = in_row_ref[...] - out_row_ref[...]
        tall = dot(spread_ref[...], wout_ref[...], 0, 0).astype(BF16)
        band = jnp.zeros(gap.shape, F32)
        for tap_row in range(3):
            band = jnp.where(gap == tap_row - 2, dot(tall, picks_ref[tap_row], 1, 1), band)
        band_ref[...] = band.astype(BF16)


def to_planes(cells):
    tiles, chans = cells[0].shape
    none = jnp.zeros((1, chans), F32)
    d0 = jnp.concatenate([none, cells[3][: tiles - 1]], axis=0)
    d1, d2, d3, d4 = cells
    d5 = jnp.concatenate([cells[0][1:], none], axis=0)
    s1, s3 = PT_A * d1, PT_A * d3
    even_a, odd_a = d4 - 2.0 * d2, s3 - 2.0 * s1
    even_b, odd_b = d4 - 0.5 * d2, 2.0 * s3 - s1
    return (
        (d0 + d4) - 2.5 * d2,
        even_a + odd_a,
        even_a - odd_a,
        even_b + odd_b,
        even_b - odd_b,
        (d1 + d5) - 2.5 * d3,
    )


def from_planes(m0, ap, an, bp, bn, m5):
    sum_a, dif_a, sum_b, dif_b = ap + an, PT_A * (ap - an), bp + bn, PT_B * (bp - bn)
    return (
        m0 + sum_a + sum_b,
        dif_a + dif_b,
        0.5 * sum_a + 2.0 * sum_b,
        0.5 * dif_a + 2.0 * dif_b + m5,
    )


def from_planes_back(m0, ap, an, bp, bn, m5):
    sum_a, dif_a, sum_b, dif_b = ap + an, PT_A * (ap - an), bp + bn, PT_B * (bp - bn)
    return (
        m0 - 2.0 * sum_a - 0.5 * sum_b,
        -(2.0 * dif_a + 0.5 * dif_b),
        -(sum_a + sum_b),
        m5 - (dif_a + dif_b),
    )


def chunks_of(rows):
    return [(low, min(low + CHUNK, rows)) for low in range(0, rows, CHUNK)]


def decoder_kernel(step_ref, me_ref, *refs, parts, rows, lat, cols):
    blocks = refs[:parts]
    (table_ref, gather_ref, scatter_ref, win_ref, bin_ref, wback_ref, bmid_ref, head_ref,
     wmid_hbm, planes_hbm, out_ref, lat_ref, slope_ref, wmid_ref, planes_ref, high_ref, rest_ref,
     q_ref, lg_ref, sems, *bufs) = refs[parts:]
    tiles = cols // TILE
    chans = wmid_ref.shape[1]
    hidden_rows, mixed_rows, grad_rows = rows + 6, rows + 4, rows + 2
    mixed_chunks, grad_chunks = chunks_of(mixed_rows), chunks_of(grad_rows)
    v1_refs, bufs = bufs[: len(mixed_chunks)], bufs[len(mixed_chunks) :]
    v2_refs, bufs = bufs[: len(grad_chunks)], bufs[len(grad_chunks) :]
    hg_refs, m_refs = bufs[: len(grad_chunks)], bufs[len(grad_chunks) :]

    copies = {}
    order = [("mid", 3 * tap_row + tap_col) for tap_col in (0, 2) for tap_row in range(3)]
    order += [("plane", plane) for plane in range(4)]
    for number, (kind, index) in enumerate(order):
        source, target = (wmid_hbm, wmid_ref) if kind == "mid" else (planes_hbm, planes_ref)
        place = index if kind == "plane" else (index // 3) * 2 + (index % 3) // 2
        copies[kind, index] = pltpu.make_async_copy(
            source.at[index], target.at[place], sems.at[number]
        )
        copies[kind, index].start()

    me = me_ref[0]
    inside_top = jnp.where(me == 0, 0.0, 1.0).astype(F32)
    inside_bottom = jnp.where(me == parts - 1, 0.0, 1.0).astype(F32)
    root_a, root_b = roots(table_ref, step_ref[0])
    total = blocks[0][...].astype(F32)
    for block in blocks[1:]:
        total = total + block[...].astype(F32)
    latent = (total / root_a).astype(BF16)
    lat_rows = (rows + 2 * HALO) * lat
    for tap_col in range(3):
        lat_ref[tap_col, 0:lat_rows, :] = dot(latent, gather_ref[tap_col], 1, 0)
        lat_ref[tap_col, lat_rows:, :] = jnp.zeros((8, cols), F32)

    def edge(row, margin, total_rows, value):
        if row < margin:
            return value * inside_top
        if row >= total_rows - margin:
            return value * inside_bottom
        return value

    def spans(low, step=None):
        step = step or LANES
        return slice(low, min(low + step, chans))

    def put_planes(cells, row, chunks, targets, lanes):
        for plane, value in enumerate(to_planes(cells)):
            value = value.astype(BF16)
            for (low, high), target in zip(chunks, targets):
                if low <= row < high + 2:
                    target[plane, (row - low) * tiles : (row - low + 1) * tiles, lanes] = value

    def hidden_piece(row, lanes):
        def run():
            window = jnp.concatenate(
                [lat_ref[tap_col, lat * row : lat * row + 16, :] for tap_col in range(3)], axis=0
            ).astype(BF16)
            pre = dot(window, win_ref[:, lanes], 0, 0) + bin_ref[:, lanes]
            sig = 0.5 + 0.5 * jnp.tanh(0.5 * pre)
            act = pre * sig
            if 2 <= row < 2 + grad_rows:
                slope_ref[(row - 2) * cols : (row - 1) * cols, lanes] = sig + act * (1.0 - sig)
            act = edge(row, 3, hidden_rows, act)
            cells = [act[part * tiles : (part + 1) * tiles] for part in range(TILE)]
            put_planes(cells, row, mixed_chunks, v1_refs, lanes)

        return run

    def mixed_piece(buf, row, base, lanes):
        def run():
            span = slice((row - base) * tiles, (row - base + 1) * tiles)
            cells = from_planes(*[buf[plane, span, lanes] for plane in range(6)])
            grads = []
            for cell in cells:
                pre = cell + bmid_ref[:, lanes]
                sig = 0.5 + 0.5 * jnp.tanh(0.5 * pre)
                grad = head_ref[:, lanes] * (sig * (1.0 + pre * (1.0 - sig)))
                grads.append(edge(row, 2, mixed_rows, grad))
            put_planes(grads, row, grad_chunks, v2_refs, lanes)

        return run

    def grad_piece(buf, row, base, target, lanes):
        def run():
            span = slice((row - base) * tiles, (row - base + 1) * tiles)
            cells = from_planes_back(*[buf[plane, span, lanes] for plane in range(6)])
            for part, cell in enumerate(cells):
                low = row * cols + part * tiles
                value = edge(row, 1, grad_rows, cell * slope_ref[low : low + tiles, lanes])
                low = (row - base) * cols + part * tiles
                target[low : low + tiles, lanes] = value.astype(BF16)

        return run

    def back_piece(row, base, target):
        def run():
            taps = dot(wback_ref[...], target[(row - base) * cols : (row - base + 1) * cols], 1, 1)
            for tap_col in range(3):
                part = taps[16 * tap_col : 16 * tap_col + 16]
                high = part.astype(BF16)
                rest = (part - high.astype(F32)).astype(BF16)
                span = slice(tap_col * cols, (tap_col + 1) * cols)
                high_ref[16 * row : 16 * row + 16, span] = high
                rest_ref[16 * row : 16 * row + 16, span] = rest

        return run

    lane_parts = [spans(low) for low in range(0, chans, LANES)]
    queue = []
    for row in range(hidden_rows):
        queue += [(("hidden", row), -1, hidden_piece(row, lanes)) for lanes in lane_parts]
    for number, (low, high) in enumerate(mixed_chunks):
        buf = m_refs[number % len(m_refs)]
        for row in range(low, high):
            queue += [
                (("mixed", row), number, mixed_piece(buf, row, low, lanes)) for lanes in lane_parts
            ]
    for index, (low, high) in enumerate(grad_chunks):
        number = len(mixed_chunks) + index
        buf, target = m_refs[number % len(m_refs)], hg_refs[index]
        for row in range(low, high):
            queue += [
                (("grad", row), number, grad_piece(buf, row, low, target, lanes))
                for lanes in lane_parts
            ]
            queue.append((("back", row), number, back_piece(row, low, target)))
    queue.reverse()

    def flush(needed):
        while any(needed(item) for item in queue):
            queue.pop()[2]()

    waited = set()

    def weights(kind, index):
        if (kind, index) not in waited:
            waited.add((kind, index))
            copies[kind, index].wait()
        if kind == "plane":
            return None
        return wmid_ref[(index // 3) * 2 + (index % 3) // 2]

    def conv(step, chunk, source, back):
        low, high = chunk
        count = (high - low) * tiles
        buf = m_refs[step % len(m_refs)]
        for plane in (0, 5, 1, 2, 3, 4):
            kerns = []
            for shift in range(3):
                tap_row = 2 - shift if back else shift
                if plane in (0, 5):
                    first = (plane == 0) != back
                    kerns.append(weights("mid", 3 * tap_row + (0 if first else 2)))
                else:
                    which = (plane - 1) ^ 2 if back else plane - 1
                    weights("plane", which)
                    kerns.append(planes_ref[which, tap_row])
            lhs = jnp.concatenate(
                [source[plane, shift * tiles : shift * tiles + count, :] for shift in range(3)], axis=1
            )
            buf[plane, 0:count, :] = dot(
                lhs, jnp.concatenate(kerns, axis=0 if back else 1), 1, 0 if back else 1
            )
            budget = QUOTA
            while budget > 0 and queue and queue[-1][1] < step:
                budget -= {"hidden": 1.0, "mixed": 1.0, "grad": 0.5, "back": 0.5}[queue[-1][0][0]]
                queue.pop()[2]()

    step = 0
    for chunk, source in zip(mixed_chunks, v1_refs):
        reach = chunk[1] + 2
        flush(lambda item: item[0][0] == "hidden" and item[0][1] < reach)
        flush(lambda item: 0 <= item[1] <= step - len(m_refs))
        conv(step, chunk, source, False)
        step += 1
    for chunk, source in zip(grad_chunks, v2_refs):
        reach = chunk[1] + 2
        flush(lambda item: item[0][0] == "mixed" and item[0][1] < reach)
        flush(lambda item: 0 <= item[1] <= step - len(m_refs))
        conv(step, chunk, source, True)
        step += 1
    flush(lambda item: True)

    q_ref[...] = dot(high_ref[...], scatter_ref[...], 1, 0) + dot(
        rest_ref[...], scatter_ref[...], 1, 0
    )
    for row in range(rows):
        lg_ref[lat * row : lat * row + lat, :] = (
            q_ref[16 * (row + 2) : 16 * (row + 2) + lat, :]
            + q_ref[16 * (row + 1) + lat : 16 * (row + 1) + 2 * lat, :]
            + q_ref[16 * row + 2 * lat : 16 * row + 3 * lat, :]
        )
    out_ref[...] = (-(root_b / root_a) * lg_ref[...]).astype(BF16)


def fill_windows(noise_ref, win_ref, lat):
    tall, cols = noise_ref.shape
    noise = noise_ref[...].astype(F32)
    spot = lax.broadcasted_iota(jnp.int32, (tall, cols), 1)
    none = jnp.zeros((lat, cols), F32)
    moved = (
        jnp.where(spot == cols - 1, 0.0, pltpu.roll(noise, cols - 1, 1)),
        noise,
        jnp.where(spot == 0, 0.0, pltpu.roll(noise, 1, 1)),
    )
    for tap_col in range(3):
        win_ref[tap_col, 0:lat, :] = none
        win_ref[tap_col, lat : lat + tall, :] = moved[tap_col]
        win_ref[tap_col, lat + tall :, :] = none


def window_of(win_ref, block, lat):
    low = block * BLOCK * lat
    group = (BLOCK + 2) * lat
    return jnp.concatenate(
        [win_ref[tap_col, low : low + group, :] for tap_col in range(3)], axis=0
    ).astype(BF16)


def weight_kernel(
    feat_ref, noise_ref, picks_ref, out_row_ref, in_row_ref, out_ref, win_ref, *, lat
):
    channels, height, cols = feat_ref.shape
    fill_windows(noise_ref, win_ref, lat)
    total = None
    for block in range(height // BLOCK):
        feats = feat_ref[:, block * BLOCK : (block + 1) * BLOCK, :]
        part = dot(feats.reshape(channels * BLOCK, cols), window_of(win_ref, block, lat), 1, 1)
        total = part if total is None else total + part
    gap = in_row_ref[...] - out_row_ref[...]
    result = jnp.zeros(out_ref.shape, F32)
    for tap_row in range(3):
        kept = jnp.where(gap == tap_row - 2, total, 0.0)
        summed = jnp.sum(kept.reshape(channels, BLOCK, -1), axis=1)
        high = summed.astype(BF16)
        rest = summed - high.astype(F32)
        mid = rest.astype(BF16)
        low = (rest - mid.astype(F32)).astype(BF16)
        for piece in (high, mid, low):
            result = result + dot(piece, picks_ref[tap_row], 1, 0)
    out_ref[...] = result


def feature_kernel(band_ref, noise_ref, out_ref, win_ref, *, lat):
    channels, height, cols = out_ref.shape
    fill_windows(noise_ref, win_ref, lat)
    for block in range(height // BLOCK):
        value = dot(band_ref[...], window_of(win_ref, block, lat), 1, 0)
        out_ref[:, block * BLOCK : (block + 1) * BLOCK, :] = value.astype(BF16).reshape(
            channels, BLOCK, cols
        )


VMEM = pl.BlockSpec(memory_space=pltpu.VMEM)
SMEM = pl.BlockSpec(memory_space=pltpu.SMEM)
PARAMS = pltpu.CompilerParams(vmem_limit_bytes=60 * 2**20)


def call(kernel, scalars, operands, outs, scratch, name, left=()):
    return pl.pallas_call(
        kernel,
        in_specs=[SMEM] * len(scalars)
        + [VMEM] * len(operands)
        + [pl.BlockSpec(memory_space=pl.ANY)] * len(left),
        out_specs=jax.tree.map(lambda _: VMEM, outs),
        out_shape=outs,
        scratch_shapes=scratch,
        compiler_params=PARAMS,
        name=name,
    )(*scalars, *operands, *left)


def body(features, w_out, noisy_latent, timestep, w_in, b_in, w_mid, b_mid, reward_head):
    _, channels, height, cols = features.shape
    lat, rows = noisy_latent.shape[1:3]
    chans = w_mid.shape[1]
    tiles = cols // TILE
    parts, images = lax.axis_size("mp"), lax.axis_size("dp")
    feats = features[0]
    me = lax.axis_index("mp").astype(jnp.int32).reshape(1)
    table = jnp.asarray(schedule_table())
    picks, spread, out_row, in_row = band_tables(channels, lat)
    picks, spread = jnp.asarray(picks, BF16), jnp.asarray(spread, BF16)
    gather, scatter = (jnp.asarray(part, BF16) for part in column_tables(cols))
    tall, deep = 3 * (BLOCK + 2) * lat, channels * BLOCK
    block_rows = (rows + 2 * HALO) * lat

    blocks = call(
        functools.partial(eps_kernel, parts=parts, rows=rows, height=height, lat=lat),
        (timestep, me),
        (feats, w_out, noisy_latent, table, picks, spread, out_row[:, None], in_row[None, :]),
        [jax.ShapeDtypeStruct((block_rows, cols), BF16) for _ in range(parts)],
        [
            pltpu.VMEM((3, (height + 2) * lat, cols), F32),
            pltpu.VMEM(((height + 2 * HALO) * lat, cols), F32),
            pltpu.VMEM((rows * lat, cols), F32),
        ],
        "eps_partial",
    )
    moved = [blocks[0]] + [
        lax.ppermute(blocks[part], "mp", [(i, i ^ part) for i in range(parts)])
        for part in range(1, parts)
    ]
    splits = 2
    once = [w_out, picks, spread, out_row[None, :], in_row[:, None]]
    planes, band = pl.pallas_call(
        prep_kernel,
        grid=(3, splits),
        in_specs=[pl.BlockSpec((3, chans // splits, chans), lambda tap_row, part: (tap_row, part, 0))]
        + [pl.BlockSpec(one.shape, lambda *_, ndim=one.ndim: (0,) * ndim) for one in once],
        out_specs=[
            pl.BlockSpec((4, 1, chans // splits, chans), lambda tap_row, part: (0, tap_row, part, 0)),
            pl.BlockSpec((deep, tall), lambda *_: (0, 0)),
        ],
        out_shape=[
            jax.ShapeDtypeStruct((4, 3, chans, chans), BF16),
            jax.ShapeDtypeStruct((deep, tall), BF16),
        ],
        compiler_params=PARAMS,
        name="weight_planes",
    )(w_mid, *once)
    taps = w_in.reshape(3, 3, chans, lat)
    win = jnp.pad(
        jnp.transpose(taps, (1, 0, 3, 2)).reshape(3, 3 * lat, chans), ((0, 0), (0, 16 - 3 * lat), (0, 0))
    ).reshape(48, chans)
    mixed_chunks, grad_chunks = chunks_of(rows + 4), chunks_of(rows + 2)
    tall_rows = [(high - low + 2) * tiles for low, high in mixed_chunks]
    back_rows = [(high - low + 2) * tiles for low, high in grad_chunks]
    noise = call(
        functools.partial(decoder_kernel, parts=parts, rows=rows, lat=lat, cols=cols),
        (timestep, me),
        (*moved, table, gather, scatter, win, b_in[None, :], win, b_mid[None, :],
         reward_head[None, :]),
        jax.ShapeDtypeStruct((rows * lat, cols), BF16),
        [
            pltpu.VMEM((3, block_rows + 8, cols), F32),
            pltpu.VMEM(((rows + 2) * cols, chans), F32),
            pltpu.VMEM((6, chans, chans), BF16),
            pltpu.VMEM((4, 3, chans, chans), BF16),
            pltpu.VMEM(((rows + 2) * 16, 3 * cols), BF16),
            pltpu.VMEM(((rows + 2) * 16, 3 * cols), BF16),
            pltpu.VMEM(((rows + 2) * 16, cols), F32),
            pltpu.VMEM((rows * lat, cols), F32),
            pltpu.SemaphoreType.DMA((10,)),
        ]
        + [pltpu.VMEM((6, size, chans), BF16) for size in tall_rows + back_rows]
        + [pltpu.VMEM(((high - low) * cols, chans), BF16) for low, high in grad_chunks]
        + [pltpu.VMEM((6, CHUNK * tiles, chans), F32) for _ in range(3)],
        "decoder",
        (w_mid, planes),
    )
    full = lax.all_gather(noise, "mp", axis=0, tiled=True)
    weight_grad = call(
        functools.partial(weight_kernel, lat=lat),
        (),
        (feats, full, picks, out_row[None, :], in_row[:, None]),
        jax.ShapeDtypeStruct((channels, 9 * lat), F32),
        [pltpu.VMEM((3, (height + 2) * lat, cols), F32)],
        "weight_grad",
    )
    stage = 1
    while stage < images:
        weight_grad = weight_grad + lax.ppermute(
            weight_grad, "dp", [(i, i ^ stage) for i in range(images)]
        )
        stage *= 2
    feature_grads = call(
        functools.partial(feature_kernel, lat=lat),
        (),
        (band, full),
        jax.ShapeDtypeStruct((channels, height, cols), BF16),
        [pltpu.VMEM((3, (height + 2) * lat, cols), F32)],
        "feature_grads",
    )
    return feature_grads[None], weight_grad / (height * cols)


def solution(mesh):
    in_specs = (
        P("dp", "mp", None, None),
        P("mp", None),
        P("dp", None, "mp", None),
        P("dp"),
        P(),
        P(),
        P(),
        P(),
        P(),
    )
    out_specs = (P("dp", "mp", None, None), P("mp", None))
    return jax.shard_map(body, mesh=mesh, in_specs=in_specs, out_specs=out_specs, check_vma=False)
```

```python
import functools

import jax
import jax.numpy as jnp
import numpy as np
from jax import lax
from jax.experimental import pallas as pl
from jax.experimental.pallas import tpu as pltpu
from jax.sharding import PartitionSpec as P

BLOCK = 16
WIDE = 32
HALO = 4
TILE = 4
PT_A = 0.5**0.5
PT_B = 2.0**0.5
STEPS = 1000
CHUNK = 9
LANES = 256
PREP_ROWS = 32
QUOTA = 4.5
F32 = jnp.float32
BF16 = jnp.bfloat16


def dot(lhs, rhs, lhs_dim, rhs_dim):
    return lax.dot_general(
        lhs, rhs, (((lhs_dim,), (rhs_dim,)), ((), ())), preferred_element_type=F32
    )


def schedule_table():
    betas = np.linspace(0.00085**0.5, 0.012**0.5, STEPS, dtype=np.float32) ** 2
    table = np.cumprod(np.float32(1.0) - betas, dtype=np.float32)
    return np.pad(table, (0, 1024 - STEPS)).reshape(8, 128)


def roots(table_ref, step):
    rows = lax.broadcasted_iota(jnp.int32, (8, 128), 0)
    cols = lax.broadcasted_iota(jnp.int32, (8, 128), 1)
    hit = jnp.where(rows * 128 + cols == step, table_ref[...], 0.0)
    level = jnp.sum(jnp.sum(hit, axis=1, keepdims=True), axis=0, keepdims=True)
    return jnp.sqrt(level), jnp.sqrt(1.0 - level)


def band_tables(channels, lat):
    wide = BLOCK + 2
    tall = 3 * wide * lat
    picks = np.zeros((3, tall, 9 * lat), np.float32)
    for tap_row in range(3):
        for tap_col in range(3):
            for row in range(wide):
                for chan in range(lat):
                    spot = (tap_col * wide + row) * lat + chan
                    picks[tap_row, spot, (3 * tap_row + tap_col) * lat + chan] = 1.0
    spread = np.kron(np.eye(channels, dtype=np.float32), np.ones((1, BLOCK), np.float32))
    out_row = np.tile(np.repeat(np.arange(wide, dtype=np.int32), lat), 3)
    in_row = np.tile(np.arange(BLOCK, dtype=np.int32), channels)
    thirds = np.concatenate([spread * (in_row % 3 == third) for third in range(3)])
    collect = np.zeros((3, 9 * lat, tall), np.float32)
    for third in range(3):
        for spot in range(tall):
            tap_row = (third - out_row[spot] + 2) % 3
            collect[third, :, spot] = picks[tap_row, spot]
    return out_row, in_row, thirds, collect


def column_tables(cols):
    tiles = cols // TILE
    place = np.arange(cols)
    source = TILE * (place % tiles) + place // tiles
    gather = np.zeros((3, cols, cols), np.float32)
    scatter = np.zeros((3, cols, cols), np.float32)
    for tap_col in range(3):
        for spot in range(cols):
            taken = source[spot] + tap_col - 1
            if 0 <= taken < cols:
                gather[tap_col, taken, spot] = 1.0
                scatter[tap_col, spot, taken] = 1.0
    return gather, scatter.reshape(3 * cols, cols)


def start_blocks(feat_hbm, feat_ref, sems):
    copies = []
    for block in range(feat_hbm.shape[1] // WIDE):
        span = slice(block * WIDE, (block + 1) * WIDE)
        copies.append(
            pltpu.make_async_copy(
                feat_hbm.at[:, span, :], feat_ref.at[:, span, :], sems.at[block]
            )
        )
        copies[-1].start()
    return copies


def pair_of(feat_ref, block):
    channels, _, cols = feat_ref.shape
    parts = [
        feat_ref[:, low : low + BLOCK, :].reshape(channels * BLOCK, cols)
        for low in range(block * WIDE, (block + 1) * WIDE, BLOCK)
    ]
    return jnp.concatenate(parts, axis=1)


def one_hot(hit):
    return jnp.where(hit, 1.0, 0.0).astype(BF16)


def banded(wout_ref, channels, lat):
    group, deep = (BLOCK + 2) * lat, channels * BLOCK
    tall = 3 * group
    place = lax.broadcasted_iota(jnp.int32, (tall, 1), 0)
    tap_col = (place >= group).astype(jnp.int32) + (place >= 2 * group).astype(jnp.int32)
    place = place - group * tap_col
    out_row = lax.div(place, jnp.full_like(place, lat))
    first = lat * tap_col + (place - lat * out_row)
    spot = lax.broadcasted_iota(jnp.int32, (1, deep), 1)
    chan = lax.div(spot, jnp.full_like(spot, BLOCK))
    gap = (spot - BLOCK * chan) - out_row
    spread = one_hot(lax.broadcasted_iota(jnp.int32, (channels, deep), 0) == chan)
    pick = lax.broadcasted_iota(jnp.int32, (tall, 9 * lat), 1)
    band = jnp.zeros((tall, deep), F32)
    for tap_row in range(3):
        taps = dot(one_hot(pick == first + 3 * lat * tap_row), wout_ref[...], 1, 0).astype(BF16)
        band = jnp.where(gap == tap_row - 2, dot(taps, spread, 1, 0), band)
    return band.astype(BF16)


def eps_kernel(step_ref, me_ref, wout_ref, noisy_ref, table_ref, feat_hbm, *refs, parts, rows, lat):
    outs = refs[:parts]
    band_ref, feat_ref, acc_ref, sum_ref, own_ref, sems = refs[parts:]
    channels, height, cols = feat_ref.shape
    copies = start_blocks(feat_hbm, feat_ref, sems)
    group = (BLOCK + 2) * lat
    band = banded(wout_ref, channels, lat)
    band_ref[...] = band
    acc_ref[...] = jnp.zeros(acc_ref.shape, F32)
    _, root_b = roots(table_ref, step_ref[0])
    edge = HALO * lat
    sum_ref[0:edge, :] = jnp.zeros((edge, cols), F32)
    sum_ref[edge + height * lat :, :] = jnp.zeros((edge, cols), F32)
    for chan in range(lat):
        own_ref[pl.ds(chan, rows, stride=lat), :] = noisy_ref[0, chan]
    for pair, copy in enumerate(copies):
        copy.wait()
        part = dot(band, pair_of(feat_ref, pair), 1, 0)
        for half in range(WIDE // BLOCK):
            low = (pair * WIDE + half * BLOCK) * lat
            span = slice(half * cols, (half + 1) * cols)
            for tap_col in range(3):
                acc_ref[tap_col, low : low + group, :] += part[
                    tap_col * group : (tap_col + 1) * group, span
                ]
    spot = lax.broadcasted_iota(jnp.int32, (height * lat, cols), 1)
    inner = slice(lat, lat + height * lat)
    left = jnp.where(spot == 0, 0.0, pltpu.roll(acc_ref[0, inner, :], 1, 1))
    right = jnp.where(spot == cols - 1, 0.0, pltpu.roll(acc_ref[2, inner, :], cols - 1, 1))
    eps = left + acc_ref[1, inner, :] + right
    sum_ref[edge : edge + height * lat, :] = -root_b * eps
    me = me_ref[0]
    low = pl.multiple_of(me * (rows * lat) + edge, 16)
    sum_ref[pl.ds(low, rows * lat), :] += own_ref[...]
    for part in range(parts):
        low = pl.multiple_of((me ^ part) * (rows * lat), 16)
        outs[part][...] = sum_ref[pl.ds(low, (rows + 2 * HALO) * lat), :].astype(BF16)


def prep_kernel(band_ref, wmid_hbm, planes_ref, wmid_ref, band_back_ref, sems):
    chans = wmid_ref.shape[1]
    copies = []
    for tap in range(9):
        copies.append(pltpu.make_async_copy(wmid_hbm.at[tap], wmid_ref.at[tap], sems.at[tap]))
        copies[-1].start()
    band_back_ref[...] = band_ref[...].T
    for tap_row in range(3):
        for tap in range(3 * tap_row, 3 * tap_row + 3):
            copies[tap].wait()
        for low in range(0, chans, PREP_ROWS):
            span = slice(low, low + PREP_ROWS)
            first = wmid_ref[3 * tap_row, span].astype(F32)
            mid = wmid_ref[3 * tap_row + 1, span].astype(F32)
            last = wmid_ref[3 * tap_row + 2, span].astype(F32)
            even = (-2.0 / 3.0) * first + (-1.0 / 3.0) * last
            odd = (-2.0 / 3.0 * PT_A) * mid
            planes_ref[0, tap_row, span] = (even + odd).astype(BF16)
            planes_ref[1, tap_row, span] = (even - odd).astype(BF16)
            even = (1.0 / 6.0) * first + (1.0 / 3.0) * last
            odd = (1.0 / 6.0 * PT_B) * mid
            planes_ref[2, tap_row, span] = (even + odd).astype(BF16)
            planes_ref[3, tap_row, span] = (even - odd).astype(BF16)


def to_planes(cells):
    tiles, chans = cells[0].shape
    none = jnp.zeros((1, chans), F32)
    d0 = jnp.concatenate([none, cells[3][: tiles - 1]], axis=0)
    d1, d2, d3, d4 = cells
    d5 = jnp.concatenate([cells[0][1:], none], axis=0)
    s1, s3 = PT_A * d1, PT_A * d3
    even_a, odd_a = d4 - 2.0 * d2, s3 - 2.0 * s1
    even_b, odd_b = d4 - 0.5 * d2, 2.0 * s3 - s1
    return (
        (d0 + d4) - 2.5 * d2,
        even_a + odd_a,
        even_a - odd_a,
        even_b + odd_b,
        even_b - odd_b,
        (d1 + d5) - 2.5 * d3,
    )


def from_planes(m0, ap, an, bp, bn, m5):
    sum_a, dif_a, sum_b, dif_b = ap + an, PT_A * (ap - an), bp + bn, PT_B * (bp - bn)
    return (
        m0 + sum_a + sum_b,
        dif_a + dif_b,
        0.5 * sum_a + 2.0 * sum_b,
        0.5 * dif_a + 2.0 * dif_b + m5,
    )


def from_planes_back(m0, ap, an, bp, bn, m5):
    sum_a, dif_a, sum_b, dif_b = ap + an, PT_A * (ap - an), bp + bn, PT_B * (bp - bn)
    return (
        m0 - 2.0 * sum_a - 0.5 * sum_b,
        -(2.0 * dif_a + 0.5 * dif_b),
        -(sum_a + sum_b),
        m5 - (dif_a + dif_b),
    )


def chunks_of(rows):
    return [(low, min(low + CHUNK, rows)) for low in range(0, rows, CHUNK)]


def decoder_kernel(step_ref, me_ref, *refs, parts, rows, lat, cols):
    blocks = refs[:parts]
    (table_ref, gather_ref, scatter_ref, taps_ref, bin_ref, bmid_ref, head_ref,
     wmid_ref, planes_ref, out_ref, lat_ref, slope_ref, high_ref, rest_ref, q_ref, lg_ref,
     tapf_ref, win_ref, *bufs) = refs[parts:]
    tiles = cols // TILE
    chans = wmid_ref.shape[1]
    hidden_rows, mixed_rows, grad_rows = rows + 6, rows + 4, rows + 2
    mixed_chunks, grad_chunks = chunks_of(mixed_rows), chunks_of(grad_rows)
    v1_refs, bufs = bufs[: len(mixed_chunks)], bufs[len(mixed_chunks) :]
    v2_refs, bufs = bufs[: len(grad_chunks)], bufs[len(grad_chunks) :]
    hg_refs, m_refs = bufs[: len(grad_chunks)], bufs[len(grad_chunks) :]

    tapf_ref[...] = jnp.zeros(tapf_ref.shape, F32)
    for tap_row in range(3):
        for tap_col in range(3):
            low = 16 * tap_col + lat * tap_row
            tapf_ref[low : low + lat, :] = taps_ref[3 * tap_row + tap_col].astype(F32)
    win_ref[...] = tapf_ref[...].astype(BF16)

    me = me_ref[0]
    inside_top = jnp.where(me == 0, 0.0, 1.0).astype(F32)
    inside_bottom = jnp.where(me == parts - 1, 0.0, 1.0).astype(F32)
    root_a, root_b = roots(table_ref, step_ref[0])
    total = blocks[0][...].astype(F32)
    for block in blocks[1:]:
        total = total + block[...].astype(F32)
    latent = (total / root_a).astype(BF16)
    lat_rows = (rows + 2 * HALO) * lat
    for tap_col in range(3):
        lat_ref[tap_col, 0:lat_rows, :] = dot(latent, gather_ref[tap_col], 1, 0)
        lat_ref[tap_col, lat_rows:, :] = jnp.zeros((8, cols), F32)

    def edge(row, margin, total_rows, value):
        if row < margin:
            return value * inside_top
        if row >= total_rows - margin:
            return value * inside_bottom
        return value

    def spans(low, step=None):
        step = step or LANES
        return slice(low, min(low + step, chans))

    def put_planes(cells, row, chunks, targets, lanes):
        for plane, value in enumerate(to_planes(cells)):
            value = value.astype(BF16)
            for (low, high), target in zip(chunks, targets):
                if low <= row < high + 2:
                    target[plane, (row - low) * tiles : (row - low + 1) * tiles, lanes] = value

    def hidden_piece(row, lanes):
        def run():
            window = jnp.concatenate(
                [lat_ref[tap_col, lat * row : lat * row + 16, :] for tap_col in range(3)], axis=0
            ).astype(BF16)
            pre = dot(window, win_ref[:, lanes], 0, 0) + bin_ref[:, lanes]
            sig = 0.5 + 0.5 * jnp.tanh(0.5 * pre)
            act = pre * sig
            if 2 <= row < 2 + grad_rows:
                slope_ref[(row - 2) * cols : (row - 1) * cols, lanes] = (
                    sig + act * (1.0 - sig)
                ).astype(BF16)
            act = edge(row, 3, hidden_rows, act)
            cells = [act[part * tiles : (part + 1) * tiles] for part in range(TILE)]
            put_planes(cells, row, mixed_chunks, v1_refs, lanes)

        return run

    def mixed_piece(buf, row, base, lanes):
        def run():
            span = slice((row - base) * tiles, (row - base + 1) * tiles)
            cells = from_planes(*[buf[plane, span, lanes] for plane in range(6)])
            grads = []
            for cell in cells:
                pre = cell + bmid_ref[:, lanes]
                sig = 0.5 + 0.5 * jnp.tanh(0.5 * pre)
                grad = head_ref[:, lanes] * (sig * (1.0 + pre * (1.0 - sig)))
                grads.append(edge(row, 2, mixed_rows, grad))
            put_planes(grads, row, grad_chunks, v2_refs, lanes)

        return run

    def grad_piece(buf, row, base, target, lanes):
        def run():
            span = slice((row - base) * tiles, (row - base + 1) * tiles)
            cells = from_planes_back(*[buf[plane, span, lanes] for plane in range(6)])
            for part, cell in enumerate(cells):
                low = row * cols + part * tiles
                value = edge(row, 1, grad_rows, cell * slope_ref[low : low + tiles, lanes].astype(F32))
                low = (row - base) * cols + part * tiles
                target[low : low + tiles, lanes] = value.astype(BF16)

        return run

    def back_piece(row, base, target):
        def run():
            taps = dot(win_ref[...], target[(row - base) * cols : (row - base + 1) * cols], 1, 1)
            for tap_col in range(3):
                part = taps[16 * tap_col : 16 * tap_col + 16]
                high = part.astype(BF16)
                rest = (part - high.astype(F32)).astype(BF16)
                span = slice(tap_col * cols, (tap_col + 1) * cols)
                high_ref[16 * row : 16 * row + 16, span] = high
                rest_ref[16 * row : 16 * row + 16, span] = rest

        return run

    lane_parts = [spans(low) for low in range(0, chans, LANES)]
    queue = []
    for row in range(hidden_rows):
        queue += [(("hidden", row), -1, hidden_piece(row, lanes)) for lanes in lane_parts]
    for number, (low, high) in enumerate(mixed_chunks):
        buf = m_refs[number % len(m_refs)]
        for row in range(low, high):
            queue += [
                (("mixed", row), number, mixed_piece(buf, row, low, lanes)) for lanes in lane_parts
            ]
    for index, (low, high) in enumerate(grad_chunks):
        number = len(mixed_chunks) + index
        buf, target = m_refs[number % len(m_refs)], hg_refs[index]
        for row in range(low, high):
            queue += [
                (("grad", row), number, grad_piece(buf, row, low, target, lanes))
                for lanes in lane_parts
            ]
            queue.append((("back", row), number, back_piece(row, low, target)))
    queue.reverse()

    def flush(needed):
        while any(needed(item) for item in queue):
            queue.pop()[2]()

    def conv(step, chunk, source, back):
        low, high = chunk
        count = (high - low) * tiles
        buf = m_refs[step % len(m_refs)]
        for plane in (0, 5, 1, 2, 3, 4):
            kerns = []
            for shift in range(3):
                tap_row = 2 - shift if back else shift
                if plane in (0, 5):
                    first = (plane == 0) != back
                    kerns.append(wmid_ref[3 * tap_row + (0 if first else 2)])
                else:
                    which = (plane - 1) ^ 2 if back else plane - 1
                    kerns.append(planes_ref[which, tap_row])
            lhs = jnp.concatenate(
                [source[plane, shift * tiles : shift * tiles + count, :] for shift in range(3)], axis=1
            )
            buf[plane, 0:count, :] = dot(
                lhs, jnp.concatenate(kerns, axis=0 if back else 1), 1, 0 if back else 1
            )
            budget = QUOTA
            while budget > 0 and queue and queue[-1][1] < step:
                budget -= {"hidden": 1.0, "mixed": 1.0, "grad": 0.5, "back": 0.5}[queue[-1][0][0]]
                queue.pop()[2]()

    step = 0
    for chunk, source in zip(mixed_chunks, v1_refs):
        reach = chunk[1] + 2
        flush(lambda item: item[0][0] == "hidden" and item[0][1] < reach)
        flush(lambda item: 0 <= item[1] <= step - len(m_refs))
        conv(step, chunk, source, False)
        step += 1
    for chunk, source in zip(grad_chunks, v2_refs):
        reach = chunk[1] + 2
        flush(lambda item: item[0][0] == "mixed" and item[0][1] < reach)
        flush(lambda item: 0 <= item[1] <= step - len(m_refs))
        conv(step, chunk, source, True)
        step += 1
    flush(lambda item: True)

    q_ref[...] = dot(high_ref[...], scatter_ref[...], 1, 0) + dot(
        rest_ref[...], scatter_ref[...], 1, 0
    )
    for row in range(rows):
        lg_ref[lat * row : lat * row + lat, :] = (
            q_ref[16 * (row + 2) : 16 * (row + 2) + lat, :]
            + q_ref[16 * (row + 1) + lat : 16 * (row + 1) + 2 * lat, :]
            + q_ref[16 * row + 2 * lat : 16 * row + 3 * lat, :]
        )
    out_ref[...] = (-(root_b / root_a) * lg_ref[...]).astype(BF16)


def fill_windows(noise_ref, win_ref, lat):
    tall, cols = noise_ref.shape
    noise = noise_ref[...].astype(F32)
    spot = lax.broadcasted_iota(jnp.int32, (tall, cols), 1)
    none = jnp.zeros((lat, cols), F32)
    moved = (
        jnp.where(spot == cols - 1, 0.0, pltpu.roll(noise, cols - 1, 1)),
        noise,
        jnp.where(spot == 0, 0.0, pltpu.roll(noise, 1, 1)),
    )
    for tap_col in range(3):
        win_ref[tap_col, 0:lat, :] = none
        win_ref[tap_col, lat : lat + tall, :] = moved[tap_col]
        win_ref[tap_col, lat + tall :, :] = none


def window_of(win_ref, block, lat):
    group = (BLOCK + 2) * lat
    parts = []
    for low in range(block * WIDE * lat, (block + 1) * WIDE * lat, BLOCK * lat):
        parts.append(
            jnp.concatenate(
                [win_ref[tap_col, low : low + group, :] for tap_col in range(3)], axis=0
            )
        )
    return jnp.concatenate(parts, axis=1).astype(BF16)


def weight_kernel(
    noise_ref, thirds_ref, collect_ref, out_row_ref, in_row_ref, feat_ref, out_ref, win_ref, *, lat
):
    channels, height, _ = feat_ref.shape
    fill_windows(noise_ref, win_ref, lat)
    pairs = range(height // WIDE)
    feats = jnp.concatenate([pair_of(feat_ref, pair) for pair in pairs], axis=1)
    windows = jnp.concatenate([window_of(win_ref, pair, lat) for pair in pairs], axis=1)
    total = dot(feats, windows, 1, 1)
    gap = in_row_ref[...] - out_row_ref[...]
    kept = jnp.where((gap >= -2) & (gap <= 0), total, 0.0).astype(BF16)
    thirds = dot(thirds_ref[...], kept, 1, 0).astype(BF16)
    result = jnp.zeros(out_ref.shape, F32)
    for third in range(3):
        piece = thirds[third * channels : (third + 1) * channels]
        result = result + dot(collect_ref[third], piece, 1, 1)
    out_ref[...] = result


def feature_kernel(band_ref, noise_ref, out_ref, win_ref, *, lat):
    channels, _, cols = out_ref.shape
    pair = pl.program_id(0)

    @pl.when(pair == 0)
    def _():
        fill_windows(noise_ref, win_ref, lat)

    group = (BLOCK + 2) * lat
    parts = []
    for half in range(WIDE // BLOCK):
        low = pl.multiple_of((pair * WIDE + half * BLOCK) * lat, 8)
        parts.append(
            jnp.concatenate([win_ref[tap_col, pl.ds(low, group), :] for tap_col in range(3)], axis=0)
        )
    value = dot(band_ref[...], jnp.concatenate(parts, axis=1).astype(BF16), 1, 0).astype(BF16)
    for half in range(WIDE // BLOCK):
        out_ref[:, half * BLOCK : (half + 1) * BLOCK, :] = value[
            :, half * cols : (half + 1) * cols
        ].reshape(channels, BLOCK, cols)


VMEM = pl.BlockSpec(memory_space=pltpu.VMEM)
SMEM = pl.BlockSpec(memory_space=pltpu.SMEM)
ROOM = 2**20


def pinned(array):
    return pltpu.with_memory_space_constraint(jnp.asarray(array), pltpu.VMEM)


def from_hbm(array):
    return pltpu.with_memory_space_constraint(jnp.asarray(array), pltpu.HBM)


def call(kernel, scalars, operands, outs, scratch, name, left=(), room=24):
    return pl.pallas_call(
        kernel,
        in_specs=[SMEM] * len(scalars)
        + [VMEM] * len(operands)
        + [pl.BlockSpec(memory_space=pltpu.HBM)] * len(left),
        out_specs=jax.tree.map(lambda _: VMEM, outs),
        out_shape=outs,
        scratch_shapes=scratch,
        compiler_params=pltpu.CompilerParams(vmem_limit_bytes=room * ROOM),
        name=name,
    )(*scalars, *operands, *(from_hbm(one) for one in left))


def eps_call(step, me, feats, kern, noisy, parts, rows):
    channels, height, cols = feats.shape
    lat = noisy.shape[1]
    block_rows = (rows + 2 * HALO) * lat
    *blocks, band = call(
        functools.partial(eps_kernel, parts=parts, rows=rows, lat=lat),
        (step, me),
        (from_hbm(kern), from_hbm(noisy), from_hbm(schedule_table())),
        [pltpu.VMEM((block_rows, cols), BF16) for _ in range(parts)]
        + [pltpu.VMEM((3 * (BLOCK + 2) * lat, channels * BLOCK), BF16)],
        [
            pltpu.VMEM((channels, height, cols), BF16),
            pltpu.VMEM((3, (height + 2) * lat, cols), F32),
            pltpu.VMEM(((height + 2 * HALO) * lat, cols), F32),
            pltpu.VMEM((rows * lat, cols), F32),
            pltpu.SemaphoreType.DMA((height // WIDE,)),
        ],
        "eps_partial",
        (feats,),
    )
    return blocks, band


def prep_call(w_mid, band):
    chans = w_mid.shape[1]
    return call(
        prep_kernel,
        (),
        (pinned(band),),
        [pltpu.VMEM((4, 3, chans, chans), BF16), pltpu.VMEM(w_mid.shape, BF16),
         pltpu.VMEM(band.shape[::-1], BF16)],
        [pltpu.SemaphoreType.DMA((9,))],
        "weight_planes",
        (w_mid,),
    )


def decoder_call(step, me, moved, taps, b_in, b_mid, head, w_mid, planes, rows):
    lat, chans = taps.shape[1:]
    block_rows, cols = moved[0].shape
    tiles = cols // TILE
    gather, scatter = (jnp.asarray(part, BF16) for part in column_tables(cols))
    mixed_chunks, grad_chunks = chunks_of(rows + 4), chunks_of(rows + 2)
    tall_rows = [(high - low + 2) * tiles for low, high in mixed_chunks]
    back_rows = [(high - low + 2) * tiles for low, high in grad_chunks]
    return call(
        functools.partial(decoder_kernel, parts=len(moved), rows=rows, lat=lat, cols=cols),
        (step, me),
        tuple(pinned(one) for one in (
            *moved, schedule_table(), gather, scatter, taps, b_in[None, :], b_mid[None, :],
            head[None, :], w_mid, planes,
        )),
        jax.ShapeDtypeStruct((rows * lat, cols), BF16),
        [
            pltpu.VMEM((3, block_rows + 8, cols), F32),
            pltpu.VMEM(((rows + 2) * cols, chans), BF16),
            pltpu.VMEM(((rows + 2) * 16, 3 * cols), BF16),
            pltpu.VMEM(((rows + 2) * 16, 3 * cols), BF16),
            pltpu.VMEM(((rows + 2) * 16, cols), F32),
            pltpu.VMEM((rows * lat, cols), F32),
            pltpu.VMEM((48, chans), F32),
            pltpu.VMEM((48, chans), BF16),
        ]
        + [pltpu.VMEM((6, size, chans), BF16) for size in tall_rows + back_rows]
        + [pltpu.VMEM(((high - low) * cols, chans), BF16) for low, high in grad_chunks]
        + [pltpu.VMEM((6, CHUNK * tiles, chans), F32) for _ in range(3)],
        "decoder",
        room=46,
    )


def weight_call(feats, full, tables, lat):
    channels, height, cols = feats.shape
    return call(
        functools.partial(weight_kernel, lat=lat),
        (),
        (full, pinned(tables["thirds"]), pinned(tables["collect"]),
         pinned(tables["out_row"][None, :]), pinned(tables["in_row"][:, None]), pinned(feats)),
        jax.ShapeDtypeStruct((9 * lat, channels), F32),
        [pltpu.VMEM((3, (height + 2) * lat, cols), F32)],
        "weight_grad",
    )


def feature_call(band, full, channels, height, lat):
    cols = full.shape[1]
    return pl.pallas_call(
        functools.partial(feature_kernel, lat=lat),
        grid=(height // WIDE,),
        in_specs=[pl.BlockSpec(one.shape, lambda pair: (0, 0)) for one in (band, full)],
        out_specs=pl.BlockSpec((channels, WIDE, cols), lambda pair: (0, pair, 0)),
        out_shape=jax.ShapeDtypeStruct((channels, height, cols), BF16),
        scratch_shapes=[pltpu.VMEM((3, (height + 2) * lat, cols), F32)],
        compiler_params=pltpu.CompilerParams(vmem_limit_bytes=24 * ROOM),
        name="feature_grads",
    )(pinned(band), full)


def tables_of(channels, lat):
    names = ("out_row", "in_row", "thirds", "collect")
    tables = dict(zip(names, band_tables(channels, lat)))
    return {
        name: value if value.dtype == np.int32 else jnp.asarray(value, BF16)
        for name, value in tables.items()
    }


def body(features, w_out, noisy_latent, timestep, w_in, b_in, w_mid, b_mid, reward_head):
    _, channels, height, cols = features.shape
    lat, rows = noisy_latent.shape[1:3]
    parts, images = lax.axis_size("mp"), lax.axis_size("dp")
    feats, kern = features[0], w_out.T
    me = lax.axis_index("mp").astype(jnp.int32).reshape(1)
    tables = tables_of(channels, lat)
    blocks, band = eps_call(timestep, me, feats, kern, noisy_latent, parts, rows)
    moved = [blocks[0]] + [
        lax.ppermute(blocks[part], "mp", [(i, i ^ part) for i in range(parts)])
        for part in range(1, parts)
    ]
    planes, w_mid, band = prep_call(w_mid, band)
    taps = jnp.transpose(w_in, (0, 2, 1))
    noise = decoder_call(
        timestep, me, moved, taps, b_in, b_mid, reward_head, w_mid, planes, rows
    )
    full = lax.all_gather(noise, "mp", axis=0, tiled=True)
    weight_grad = weight_call(feats, full, tables, lat)
    stage = 1
    while stage < images:
        weight_grad = weight_grad + lax.ppermute(
            weight_grad, "dp", [(i, i ^ stage) for i in range(images)]
        )
        stage *= 2
    feature_grads = feature_call(band, full, channels, height, lat)
    return feature_grads[None], (weight_grad / (height * cols)).T


def solution(mesh):
    in_specs = (
        P("dp", "mp", None, None),
        P("mp", None),
        P("dp", None, "mp", None),
        P("dp"),
        P(),
        P(),
        P(),
        P(),
        P(),
    )
    out_specs = (P("dp", "mp", None, None), P("mp", None))
    return jax.shard_map(body, mesh=mesh, in_specs=in_specs, out_specs=out_specs, check_vma=False)
```

```python
import functools

import jax
import jax.numpy as jnp
import numpy as np
from jax import lax
from jax.experimental import pallas as pl
from jax.experimental.pallas import tpu as pltpu
from jax.sharding import PartitionSpec as P

BLOCK = 16
WIDE = 32
HALO = 4
TILE = 4
PT_A = 0.5**0.5
PT_B = 2.0**0.5
STEPS = 1000
CHUNK = 18
LANES = 256
PREP_ROWS = 32
QUOTA = 100.0
F32 = jnp.float32
BF16 = jnp.bfloat16


def dot(lhs, rhs, lhs_dim, rhs_dim):
    return lax.dot_general(
        lhs, rhs, (((lhs_dim,), (rhs_dim,)), ((), ())), preferred_element_type=F32
    )


def schedule_table():
    betas = np.linspace(0.00085**0.5, 0.012**0.5, STEPS, dtype=np.float32) ** 2
    table = np.cumprod(np.float32(1.0) - betas, dtype=np.float32)
    return np.pad(table, (0, 1024 - STEPS)).reshape(8, 128)


def roots(table_ref, step):
    rows = lax.broadcasted_iota(jnp.int32, (8, 128), 0)
    cols = lax.broadcasted_iota(jnp.int32, (8, 128), 1)
    hit = jnp.where(rows * 128 + cols == step, table_ref[...], 0.0)
    level = jnp.sum(jnp.sum(hit, axis=1, keepdims=True), axis=0, keepdims=True)
    return jnp.sqrt(level), jnp.sqrt(1.0 - level)


def band_tables(channels, lat):
    wide = BLOCK + 2
    tall = 3 * wide * lat
    picks = np.zeros((3, tall, 9 * lat), np.float32)
    for tap_row in range(3):
        for tap_col in range(3):
            for row in range(wide):
                for chan in range(lat):
                    spot = (tap_col * wide + row) * lat + chan
                    picks[tap_row, spot, (3 * tap_row + tap_col) * lat + chan] = 1.0
    spread = np.kron(np.eye(channels, dtype=np.float32), np.ones((1, BLOCK), np.float32))
    out_row = np.tile(np.repeat(np.arange(wide, dtype=np.int32), lat), 3)
    in_row = np.tile(np.arange(BLOCK, dtype=np.int32), channels)
    thirds = np.concatenate([spread * (in_row % 3 == third) for third in range(3)])
    collect = np.zeros((3, 9 * lat, tall), np.float32)
    for third in range(3):
        for spot in range(tall):
            tap_row = (third - out_row[spot] + 2) % 3
            collect[third, :, spot] = picks[tap_row, spot]
    return out_row, in_row, thirds, collect


def column_tables(cols):
    tiles = cols // TILE
    place = np.arange(cols)
    source = TILE * (place % tiles) + place // tiles
    gather = np.zeros((3, cols, cols), np.float32)
    scatter = np.zeros((3, cols, cols), np.float32)
    for tap_col in range(3):
        for spot in range(cols):
            taken = source[spot] + tap_col - 1
            if 0 <= taken < cols:
                gather[tap_col, taken, spot] = 1.0
                scatter[tap_col, spot, taken] = 1.0
    return gather, scatter.reshape(3 * cols, cols)


def start_blocks(feat_hbm, feat_ref, sems):
    copies = []
    for block in range(feat_hbm.shape[1] // WIDE):
        span = slice(block * WIDE, (block + 1) * WIDE)
        copies.append(
            pltpu.make_async_copy(
                feat_hbm.at[:, span, :], feat_ref.at[:, span, :], sems.at[block]
            )
        )
        copies[-1].start()
    return copies


def pair_of(feat_ref, block):
    channels, _, cols = feat_ref.shape
    parts = [
        feat_ref[:, low : low + BLOCK, :].reshape(channels * BLOCK, cols)
        for low in range(block * WIDE, (block + 1) * WIDE, BLOCK)
    ]
    return jnp.concatenate(parts, axis=1)


def one_hot(hit):
    return jnp.where(hit, 1.0, 0.0).astype(BF16)


def banded(wout_ref, channels, lat):
    group, deep = (BLOCK + 2) * lat, channels * BLOCK
    tall = 3 * group
    place = lax.broadcasted_iota(jnp.int32, (tall, 1), 0)
    tap_col = (place >= group).astype(jnp.int32) + (place >= 2 * group).astype(jnp.int32)
    place = place - group * tap_col
    out_row = lax.div(place, jnp.full_like(place, lat))
    first = lat * tap_col + (place - lat * out_row)
    spot = lax.broadcasted_iota(jnp.int32, (1, deep), 1)
    chan = lax.div(spot, jnp.full_like(spot, BLOCK))
    gap = (spot - BLOCK * chan) - out_row
    spread = one_hot(lax.broadcasted_iota(jnp.int32, (channels, deep), 0) == chan)
    pick = lax.broadcasted_iota(jnp.int32, (tall, 9 * lat), 1)
    band = jnp.zeros((tall, deep), F32)
    for tap_row in range(3):
        taps = dot(one_hot(pick == first + 3 * lat * tap_row), wout_ref[...], 1, 0).astype(BF16)
        band = jnp.where(gap == tap_row - 2, dot(taps, spread, 1, 0), band)
    return band.astype(BF16)


def eps_kernel(step_ref, me_ref, wout_ref, noisy_ref, table_ref, feat_hbm, *refs, parts, rows, lat):
    outs = refs[:parts]
    band_ref, feat_ref, acc_ref, sum_ref, own_ref, sems = refs[parts:]
    channels, height, cols = feat_ref.shape
    copies = start_blocks(feat_hbm, feat_ref, sems)
    group = (BLOCK + 2) * lat
    band = banded(wout_ref, channels, lat)
    band_ref[...] = band
    acc_ref[...] = jnp.zeros(acc_ref.shape, F32)
    _, root_b = roots(table_ref, step_ref[0])
    edge = HALO * lat
    sum_ref[0:edge, :] = jnp.zeros((edge, cols), F32)
    sum_ref[edge + height * lat :, :] = jnp.zeros((edge, cols), F32)
    for chan in range(lat):
        own_ref[pl.ds(chan, rows, stride=lat), :] = noisy_ref[0, chan]
    for pair, copy in enumerate(copies):
        copy.wait()
        part = dot(band, pair_of(feat_ref, pair), 1, 0)
        for half in range(WIDE // BLOCK):
            low = (pair * WIDE + half * BLOCK) * lat
            span = slice(half * cols, (half + 1) * cols)
            for tap_col in range(3):
                acc_ref[tap_col, low : low + group, :] += part[
                    tap_col * group : (tap_col + 1) * group, span
                ]
    spot = lax.broadcasted_iota(jnp.int32, (height * lat, cols), 1)
    inner = slice(lat, lat + height * lat)
    left = jnp.where(spot == 0, 0.0, pltpu.roll(acc_ref[0, inner, :], 1, 1))
    right = jnp.where(spot == cols - 1, 0.0, pltpu.roll(acc_ref[2, inner, :], cols - 1, 1))
    eps = left + acc_ref[1, inner, :] + right
    sum_ref[edge : edge + height * lat, :] = -root_b * eps
    me = me_ref[0]
    low = pl.multiple_of(me * (rows * lat) + edge, 16)
    sum_ref[pl.ds(low, rows * lat), :] += own_ref[...]
    for part in range(parts):
        low = pl.multiple_of((me ^ part) * (rows * lat), 16)
        outs[part][...] = sum_ref[pl.ds(low, (rows + 2 * HALO) * lat), :].astype(BF16)


def prep_kernel(band_ref, wmid_hbm, planes_ref, wmid_ref, band_back_ref, sems):
    chans = wmid_ref.shape[1]
    copies = []
    for tap in range(9):
        copies.append(pltpu.make_async_copy(wmid_hbm.at[tap], wmid_ref.at[tap], sems.at[tap]))
        copies[-1].start()
    band_back_ref[...] = band_ref[...].T
    for tap_row in range(3):
        for tap in range(3 * tap_row, 3 * tap_row + 3):
            copies[tap].wait()
        for low in range(0, chans, PREP_ROWS):
            span = slice(low, low + PREP_ROWS)
            first = wmid_ref[3 * tap_row, span].astype(F32)
            mid = wmid_ref[3 * tap_row + 1, span].astype(F32)
            last = wmid_ref[3 * tap_row + 2, span].astype(F32)
            even = (-2.0 / 3.0) * first + (-1.0 / 3.0) * last
            odd = (-2.0 / 3.0 * PT_A) * mid
            planes_ref[0, tap_row, span] = (even + odd).astype(BF16)
            planes_ref[1, tap_row, span] = (even - odd).astype(BF16)
            even = (1.0 / 6.0) * first + (1.0 / 3.0) * last
            odd = (1.0 / 6.0 * PT_B) * mid
            planes_ref[2, tap_row, span] = (even + odd).astype(BF16)
            planes_ref[3, tap_row, span] = (even - odd).astype(BF16)


def to_planes(cells):
    tiles, chans = cells[0].shape
    none = jnp.zeros((1, chans), F32)
    d0 = jnp.concatenate([none, cells[3][: tiles - 1]], axis=0)
    d1, d2, d3, d4 = cells
    d5 = jnp.concatenate([cells[0][1:], none], axis=0)
    s1, s3 = PT_A * d1, PT_A * d3
    even_a, odd_a = d4 - 2.0 * d2, s3 - 2.0 * s1
    even_b, odd_b = d4 - 0.5 * d2, 2.0 * s3 - s1
    return (
        (d0 + d4) - 2.5 * d2,
        even_a + odd_a,
        even_a - odd_a,
        even_b + odd_b,
        even_b - odd_b,
        (d1 + d5) - 2.5 * d3,
    )


def half_from_planes(m0, ap, an, bp, bn, m5):
    sum_a, dif_a = ap + an, (0.5 * PT_A) * (ap - an)
    sum_b, dif_b = bp + bn, (0.5 * PT_B) * (bp - bn)
    return (
        0.5 * (m0 + sum_a + sum_b),
        dif_a + dif_b,
        0.25 * sum_a + sum_b,
        0.5 * dif_a + 2.0 * dif_b + 0.5 * m5,
    )


def from_planes_back(m0, ap, an, bp, bn, m5):
    sum_a, dif_a, sum_b, dif_b = ap + an, PT_A * (ap - an), bp + bn, PT_B * (bp - bn)
    return (
        m0 - 2.0 * sum_a - 0.5 * sum_b,
        -(2.0 * dif_a + 0.5 * dif_b),
        -(sum_a + sum_b),
        m5 - (dif_a + dif_b),
    )


def chunks_of(rows):
    return [(low, min(low + CHUNK, rows)) for low in range(0, rows, CHUNK)]


def decoder_kernel(step_ref, me_ref, *refs, parts, rows, lat, cols):
    blocks = refs[:parts]
    (table_ref, gather_ref, scatter_ref, taps_ref, bin_ref, bmid_ref, head_ref,
     wmid_ref, planes_ref, out_ref, lat_ref, slope_ref, high_ref, rest_ref, q_ref, lg_ref,
     tapf_ref, win_ref, *bufs) = refs[parts:]
    tiles = cols // TILE
    chans = wmid_ref.shape[1]
    hidden_rows, mixed_rows, grad_rows = rows + 6, rows + 4, rows + 2
    mixed_chunks, grad_chunks = chunks_of(mixed_rows), chunks_of(grad_rows)
    v1_refs, bufs = bufs[: len(mixed_chunks)], bufs[len(mixed_chunks) :]
    v2_refs, bufs = bufs[: len(grad_chunks)], bufs[len(grad_chunks) :]
    hg_refs, m_refs = bufs[: len(grad_chunks)], bufs[len(grad_chunks) :]

    tapf_ref[...] = jnp.zeros(tapf_ref.shape, F32)
    for tap_row in range(3):
        for tap_col in range(3):
            low = 16 * tap_col + lat * tap_row
            tapf_ref[low : low + lat, :] = taps_ref[3 * tap_row + tap_col].astype(F32)
    win_ref[...] = (0.5 * tapf_ref[...]).astype(BF16)

    me = me_ref[0]
    inside_top = jnp.where(me == 0, 0.0, 1.0).astype(F32)
    inside_bottom = jnp.where(me == parts - 1, 0.0, 1.0).astype(F32)
    root_a, root_b = roots(table_ref, step_ref[0])
    total = blocks[0][...].astype(F32)
    for block in blocks[1:]:
        total = total + block[...].astype(F32)
    latent = (total / root_a).astype(BF16)
    lat_rows = (rows + 2 * HALO) * lat
    for tap_col in range(3):
        lat_ref[tap_col, 0:lat_rows, :] = dot(latent, gather_ref[tap_col], 1, 0)
        lat_ref[tap_col, lat_rows:, :] = jnp.zeros((8, cols), F32)

    def edge(row, margin, total_rows, value):
        if row < margin:
            return value * inside_top
        if row >= total_rows - margin:
            return value * inside_bottom
        return value

    def spans(low, step=None):
        step = step or LANES
        return slice(low, min(low + step, chans))

    def put_planes(cells, row, chunks, targets, lanes):
        for plane, value in enumerate(to_planes(cells)):
            value = value.astype(BF16)
            for (low, high), target in zip(chunks, targets):
                if low <= row < high + 2:
                    target[plane, (row - low) * tiles : (row - low + 1) * tiles, lanes] = value

    def hidden_piece(row, lanes):
        def run():
            window = jnp.concatenate(
                [lat_ref[tap_col, lat * row : lat * row + 16, :] for tap_col in range(3)], axis=0
            ).astype(BF16)
            half = dot(window, win_ref[:, lanes], 0, 0) + 0.5 * bin_ref[:, lanes]
            tanh = jnp.tanh(half)
            twice = 1.0 + tanh
            act = half * twice
            if 2 <= row < 2 + grad_rows:
                slope_ref[(row - 2) * cols : (row - 1) * cols, lanes] = (
                    twice + act * (1.0 - tanh)
                ).astype(BF16)
            act = edge(row, 3, hidden_rows, act)
            cells = [act[part * tiles : (part + 1) * tiles] for part in range(TILE)]
            put_planes(cells, row, mixed_chunks, v1_refs, lanes)

        return run

    def mixed_piece(buf, row, base, lanes):
        def run():
            span = slice((row - base) * tiles, (row - base + 1) * tiles)
            cells = half_from_planes(*[buf[plane, span, lanes] for plane in range(6)])
            grads = []
            for cell in cells:
                half = cell + 0.5 * bmid_ref[:, lanes]
                tanh = jnp.tanh(half)
                twice = 1.0 + tanh
                grad = (0.5 * head_ref[:, lanes]) * (twice + half * twice * (1.0 - tanh))
                grads.append(edge(row, 2, mixed_rows, grad))
            put_planes(grads, row, grad_chunks, v2_refs, lanes)

        return run

    def grad_piece(buf, row, base, target, lanes):
        def run():
            span = slice((row - base) * tiles, (row - base + 1) * tiles)
            cells = from_planes_back(*[buf[plane, span, lanes] for plane in range(6)])
            for part, cell in enumerate(cells):
                low = row * cols + part * tiles
                value = edge(row, 1, grad_rows, cell * slope_ref[low : low + tiles, lanes].astype(F32))
                low = (row - base) * cols + part * tiles
                target[low : low + tiles, lanes] = value.astype(BF16)

        return run

    def back_piece(row, base, target):
        def run():
            taps = dot(win_ref[...], target[(row - base) * cols : (row - base + 1) * cols], 1, 1)
            for tap_col in range(3):
                part = taps[16 * tap_col : 16 * tap_col + 16]
                high = part.astype(BF16)
                rest = (part - high.astype(F32)).astype(BF16)
                span = slice(tap_col * cols, (tap_col + 1) * cols)
                high_ref[16 * row : 16 * row + 16, span] = high
                rest_ref[16 * row : 16 * row + 16, span] = rest

        return run

    lane_parts = [spans(low) for low in range(0, chans, LANES)]
    queue = []
    for row in range(hidden_rows):
        queue += [(("hidden", row), -1, hidden_piece(row, lanes)) for lanes in lane_parts]
    for number, (low, high) in enumerate(mixed_chunks):
        buf = m_refs[number % len(m_refs)]
        for row in range(low, high):
            queue += [
                (("mixed", row), number, mixed_piece(buf, row, low, lanes)) for lanes in lane_parts
            ]
    for index, (low, high) in enumerate(grad_chunks):
        number = len(mixed_chunks) + index
        buf, target = m_refs[number % len(m_refs)], hg_refs[index]
        for row in range(low, high):
            queue += [
                (("grad", row), number, grad_piece(buf, row, low, target, lanes))
                for lanes in lane_parts
            ]
            queue.append((("back", row), number, back_piece(row, low, target)))
    queue.reverse()

    def flush(needed):
        while any(needed(item) for item in queue):
            queue.pop()[2]()

    def conv(step, chunk, source, back):
        low, high = chunk
        count = (high - low) * tiles
        buf = m_refs[step % len(m_refs)]
        for plane in (0, 5, 1, 2, 3, 4):
            kerns = []
            for shift in range(3):
                tap_row = 2 - shift if back else shift
                if plane in (0, 5):
                    first = (plane == 0) != back
                    kerns.append(wmid_ref[3 * tap_row + (0 if first else 2)])
                else:
                    which = (plane - 1) ^ 2 if back else plane - 1
                    kerns.append(planes_ref[which, tap_row])
            lhs = jnp.concatenate(
                [source[plane, shift * tiles : shift * tiles + count, :] for shift in range(3)], axis=1
            )
            buf[plane, 0:count, :] = dot(
                lhs, jnp.concatenate(kerns, axis=0 if back else 1), 1, 0 if back else 1
            )
            budget = QUOTA
            while budget > 0 and queue and queue[-1][1] < step:
                budget -= {"hidden": 1.0, "mixed": 1.0, "grad": 0.5, "back": 0.5}[queue[-1][0][0]]
                queue.pop()[2]()

    step = 0
    for chunk, source in zip(mixed_chunks, v1_refs):
        reach = chunk[1] + 2
        flush(lambda item: item[0][0] == "hidden" and item[0][1] < reach)
        flush(lambda item: 0 <= item[1] <= step - len(m_refs))
        conv(step, chunk, source, False)
        step += 1
    for chunk, source in zip(grad_chunks, v2_refs):
        reach = chunk[1] + 2
        flush(lambda item: item[0][0] == "mixed" and item[0][1] < reach)
        flush(lambda item: 0 <= item[1] <= step - len(m_refs))
        conv(step, chunk, source, True)
        step += 1
    flush(lambda item: True)

    q_ref[...] = dot(high_ref[...], scatter_ref[...], 1, 0) + dot(
        rest_ref[...], scatter_ref[...], 1, 0
    )
    for row in range(rows):
        lg_ref[lat * row : lat * row + lat, :] = (
            q_ref[16 * (row + 2) : 16 * (row + 2) + lat, :]
            + q_ref[16 * (row + 1) + lat : 16 * (row + 1) + 2 * lat, :]
            + q_ref[16 * row + 2 * lat : 16 * row + 3 * lat, :]
        )
    out_ref[...] = (-(root_b / root_a) * lg_ref[...]).astype(BF16)


def fill_windows(noise_ref, win_ref, lat):
    tall, cols = noise_ref.shape
    noise = noise_ref[...].astype(F32)
    spot = lax.broadcasted_iota(jnp.int32, (tall, cols), 1)
    none = jnp.zeros((lat, cols), F32)
    moved = (
        jnp.where(spot == cols - 1, 0.0, pltpu.roll(noise, cols - 1, 1)),
        noise,
        jnp.where(spot == 0, 0.0, pltpu.roll(noise, 1, 1)),
    )
    for tap_col in range(3):
        win_ref[tap_col, 0:lat, :] = none
        win_ref[tap_col, lat : lat + tall, :] = moved[tap_col]
        win_ref[tap_col, lat + tall :, :] = none


def window_of(win_ref, block, lat):
    group = (BLOCK + 2) * lat
    parts = []
    for low in range(block * WIDE * lat, (block + 1) * WIDE * lat, BLOCK * lat):
        parts.append(
            jnp.concatenate(
                [win_ref[tap_col, low : low + group, :] for tap_col in range(3)], axis=0
            )
        )
    return jnp.concatenate(parts, axis=1).astype(BF16)


def weight_kernel(
    noise_ref, thirds_ref, collect_ref, out_row_ref, in_row_ref, feat_ref, out_ref, win_ref, *, lat
):
    channels, height, _ = feat_ref.shape
    fill_windows(noise_ref, win_ref, lat)
    pairs = range(height // WIDE)
    feats = jnp.concatenate([pair_of(feat_ref, pair) for pair in pairs], axis=1)
    windows = jnp.concatenate([window_of(win_ref, pair, lat) for pair in pairs], axis=1)
    total = dot(feats, windows, 1, 1)
    gap = in_row_ref[...] - out_row_ref[...]
    kept = jnp.where((gap >= -2) & (gap <= 0), total, 0.0).astype(BF16)
    thirds = dot(thirds_ref[...], kept, 1, 0).astype(BF16)
    result = jnp.zeros(out_ref.shape, F32)
    for third in range(3):
        piece = thirds[third * channels : (third + 1) * channels]
        result = result + dot(collect_ref[third], piece, 1, 1)
    out_ref[...] = result


def feature_kernel(band_ref, noise_ref, *refs, first, lat):
    out_ref, win_ref = refs[-2:]
    channels, _, cols = out_ref.shape
    pair = pl.program_id(0) + first

    @pl.when(pl.program_id(0) == 0)
    def _():
        fill_windows(noise_ref, win_ref, lat)

    group = (BLOCK + 2) * lat
    parts = []
    for half in range(WIDE // BLOCK):
        low = pl.multiple_of((pair * WIDE + half * BLOCK) * lat, 8)
        parts.append(
            jnp.concatenate([win_ref[tap_col, pl.ds(low, group), :] for tap_col in range(3)], axis=0)
        )
    value = dot(band_ref[...], jnp.concatenate(parts, axis=1).astype(BF16), 1, 0).astype(BF16)
    for half in range(WIDE // BLOCK):
        out_ref[:, half * BLOCK : (half + 1) * BLOCK, :] = value[
            :, half * cols : (half + 1) * cols
        ].reshape(channels, BLOCK, cols)


VMEM = pl.BlockSpec(memory_space=pltpu.VMEM)
SMEM = pl.BlockSpec(memory_space=pltpu.SMEM)
ROOM = 2**20


def pinned(array):
    return pltpu.with_memory_space_constraint(jnp.asarray(array), pltpu.VMEM)


def from_hbm(array):
    return pltpu.with_memory_space_constraint(jnp.asarray(array), pltpu.HBM)


def call(kernel, scalars, operands, outs, scratch, name, left=(), room=24):
    return pl.pallas_call(
        kernel,
        in_specs=[SMEM] * len(scalars)
        + [VMEM] * len(operands)
        + [pl.BlockSpec(memory_space=pltpu.HBM)] * len(left),
        out_specs=jax.tree.map(lambda _: VMEM, outs),
        out_shape=outs,
        scratch_shapes=scratch,
        compiler_params=pltpu.CompilerParams(vmem_limit_bytes=room * ROOM),
        name=name,
    )(*scalars, *operands, *(from_hbm(one) for one in left))


def eps_call(step, me, feats, kern, noisy, parts, rows):
    channels, height, cols = feats.shape
    lat = noisy.shape[1]
    block_rows = (rows + 2 * HALO) * lat
    *blocks, band = call(
        functools.partial(eps_kernel, parts=parts, rows=rows, lat=lat),
        (step, me),
        (from_hbm(kern), from_hbm(noisy), from_hbm(schedule_table())),
        [pltpu.VMEM((block_rows, cols), BF16) for _ in range(parts)]
        + [pltpu.VMEM((3 * (BLOCK + 2) * lat, channels * BLOCK), BF16)],
        [
            pltpu.VMEM((channels, height, cols), BF16),
            pltpu.VMEM((3, (height + 2) * lat, cols), F32),
            pltpu.VMEM(((height + 2 * HALO) * lat, cols), F32),
            pltpu.VMEM((rows * lat, cols), F32),
            pltpu.SemaphoreType.DMA((height // WIDE,)),
        ],
        "eps_partial",
        (feats,),
    )
    return blocks, band


def prep_call(w_mid, band):
    chans = w_mid.shape[1]
    return call(
        prep_kernel,
        (),
        (pinned(band),),
        [pltpu.VMEM((4, 3, chans, chans), BF16), pltpu.VMEM(w_mid.shape, BF16),
         pltpu.VMEM(band.shape[::-1], BF16)],
        [pltpu.SemaphoreType.DMA((9,))],
        "weight_planes",
        (w_mid,),
    )


def decoder_call(step, me, moved, taps, b_in, b_mid, head, w_mid, planes, rows):
    lat, chans = taps.shape[1:]
    block_rows, cols = moved[0].shape
    tiles = cols // TILE
    gather, scatter = (jnp.asarray(part, BF16) for part in column_tables(cols))
    mixed_chunks, grad_chunks = chunks_of(rows + 4), chunks_of(rows + 2)
    tall_rows = [(high - low + 2) * tiles for low, high in mixed_chunks]
    back_rows = [(high - low + 2) * tiles for low, high in grad_chunks]
    return call(
        functools.partial(decoder_kernel, parts=len(moved), rows=rows, lat=lat, cols=cols),
        (step, me),
        tuple(pinned(one) for one in (
            *moved, schedule_table(), gather, scatter, taps, b_in[None, :], b_mid[None, :],
            head[None, :], w_mid, planes,
        )),
        jax.ShapeDtypeStruct((rows * lat, cols), BF16),
        [
            pltpu.VMEM((3, block_rows + 8, cols), F32),
            pltpu.VMEM(((rows + 2) * cols, chans), BF16),
            pltpu.VMEM(((rows + 2) * 16, 3 * cols), BF16),
            pltpu.VMEM(((rows + 2) * 16, 3 * cols), BF16),
            pltpu.VMEM(((rows + 2) * 16, cols), F32),
            pltpu.VMEM((rows * lat, cols), F32),
            pltpu.VMEM((48, chans), F32),
            pltpu.VMEM((48, chans), BF16),
        ]
        + [pltpu.VMEM((6, size, chans), BF16) for size in tall_rows + back_rows]
        + [pltpu.VMEM(((high - low) * cols, chans), BF16) for low, high in grad_chunks]
        + [pltpu.VMEM((6, CHUNK * tiles, chans), F32) for _ in range(3)],
        "decoder",
        room=46,
    )


def weight_call(feats, full, tables, lat):
    channels, height, cols = feats.shape
    return call(
        functools.partial(weight_kernel, lat=lat),
        (),
        (full, pinned(tables["thirds"]), pinned(tables["collect"]),
         pinned(tables["out_row"][None, :]), pinned(tables["in_row"][:, None]), pinned(feats)),
        jax.ShapeDtypeStruct((9 * lat, channels), F32),
        [pltpu.VMEM((3, (height + 2) * lat, cols), F32)],
        "weight_grad",
    )


def feature_call(band, full, channels, height, lat, first, last, before=None):
    cols = full.shape[1]
    extra = [] if before is None else [before]
    return pl.pallas_call(
        functools.partial(feature_kernel, first=first, lat=lat),
        grid=(last - first,),
        in_specs=[pl.BlockSpec(one.shape, lambda pair: (0, 0)) for one in (band, full)]
        + [pl.BlockSpec(memory_space=pltpu.HBM) for _ in extra],
        out_specs=pl.BlockSpec((channels, WIDE, cols), lambda pair: (0, pair + first, 0)),
        out_shape=jax.ShapeDtypeStruct((channels, height, cols), BF16),
        scratch_shapes=[pltpu.VMEM((3, (height + 2) * lat, cols), F32)],
        input_output_aliases={2: 0} if extra else {},
        compiler_params=pltpu.CompilerParams(vmem_limit_bytes=24 * ROOM),
        name="feature_grads",
    )(pinned(band), full, *extra)


def tables_of(channels, lat):
    names = ("out_row", "in_row", "thirds", "collect")
    tables = dict(zip(names, band_tables(channels, lat)))
    return {
        name: value if value.dtype == np.int32 else jnp.asarray(value, BF16)
        for name, value in tables.items()
    }


def body(features, w_out, noisy_latent, timestep, w_in, b_in, w_mid, b_mid, reward_head):
    _, channels, height, cols = features.shape
    lat, rows = noisy_latent.shape[1:3]
    parts, images = lax.axis_size("mp"), lax.axis_size("dp")
    feats, kern = features[0], w_out.T
    me = lax.axis_index("mp").astype(jnp.int32).reshape(1)
    tables = tables_of(channels, lat)
    blocks, band = eps_call(timestep, me, feats, kern, noisy_latent, parts, rows)
    moved = [blocks[0]] + [
        lax.ppermute(blocks[part], "mp", [(i, i ^ part) for i in range(parts)])
        for part in range(1, parts)
    ]
    planes, w_mid, band = prep_call(w_mid, band)
    taps = jnp.transpose(w_in, (0, 2, 1))
    noise = decoder_call(
        timestep, me, moved, taps, b_in, b_mid, reward_head, w_mid, planes, rows
    )
    full = lax.all_gather(noise, "mp", axis=0, tiled=True)
    weight_grad = weight_call(feats, full, tables, lat)
    pairs = height // WIDE
    stage, feature_grads = 1, None
    while stage < images:
        other = lax.ppermute(weight_grad, "dp", [(i, i ^ stage) for i in range(images)])
        if stage == 1:
            feature_grads = feature_call(band, full, channels, height, lat, 0, pairs // 2)
            other, feature_grads = lax.optimization_barrier((other, feature_grads))
        weight_grad = weight_grad + other
        stage *= 2
    feature_grads = feature_call(
        band, full, channels, height, lat, pairs // 2, pairs, feature_grads
    )
    return feature_grads[None], (weight_grad / (height * cols)).T


def solution(mesh):
    in_specs = (
        P("dp", "mp", None, None),
        P("mp", None),
        P("dp", None, "mp", None),
        P("dp"),
        P(),
        P(),
        P(),
        P(),
        P(),
    )
    out_specs = (P("dp", "mp", None, None), P("mp", None))
    return jax.shard_map(body, mesh=mesh, in_specs=in_specs, out_specs=out_specs, check_vma=False)
```

```python
import functools

import jax
import jax.numpy as jnp
import numpy as np
from jax import lax
from jax.experimental import pallas as pl
from jax.experimental.pallas import tpu as pltpu
from jax.sharding import PartitionSpec as P

BLOCK = 16
WIDE = 32
HALO = 4
TILE = 4
PT_A = 0.5**0.5
PT_B = 2.0**0.5
STEPS = 1000
CHUNK = 18
LANES = 256
PREP_ROWS = 32
QUOTA = 100.0
F32 = jnp.float32
BF16 = jnp.bfloat16


def dot(lhs, rhs, lhs_dim, rhs_dim):
    return lax.dot_general(
        lhs, rhs, (((lhs_dim,), (rhs_dim,)), ((), ())), preferred_element_type=F32
    )


def schedule_table():
    betas = np.linspace(0.00085**0.5, 0.012**0.5, STEPS, dtype=np.float32) ** 2
    table = np.cumprod(np.float32(1.0) - betas, dtype=np.float32)
    return np.pad(table, (0, 1024 - STEPS)).reshape(8, 128)


def roots(table_ref, step):
    rows = lax.broadcasted_iota(jnp.int32, (8, 128), 0)
    cols = lax.broadcasted_iota(jnp.int32, (8, 128), 1)
    hit = jnp.where(rows * 128 + cols == step, table_ref[...], 0.0)
    level = jnp.sum(jnp.sum(hit, axis=1, keepdims=True), axis=0, keepdims=True)
    return jnp.sqrt(level), jnp.sqrt(1.0 - level)


def band_tables(channels, lat):
    wide = BLOCK + 2
    tall = 3 * wide * lat
    picks = np.zeros((3, tall, 9 * lat), np.float32)
    for tap_row in range(3):
        for tap_col in range(3):
            for row in range(wide):
                for chan in range(lat):
                    spot = (tap_col * wide + row) * lat + chan
                    picks[tap_row, spot, (3 * tap_row + tap_col) * lat + chan] = 1.0
    spread = np.kron(np.eye(channels, dtype=np.float32), np.ones((1, BLOCK), np.float32))
    out_row = np.tile(np.repeat(np.arange(wide, dtype=np.int32), lat), 3)
    in_row = np.tile(np.arange(BLOCK, dtype=np.int32), channels)
    thirds = np.concatenate([spread * (in_row % 3 == third) for third in range(3)])
    collect = np.zeros((3, 9 * lat, tall), np.float32)
    for third in range(3):
        for spot in range(tall):
            tap_row = (third - out_row[spot] + 2) % 3
            collect[third, :, spot] = picks[tap_row, spot]
    return out_row, in_row, thirds, collect


def column_tables(cols):
    tiles = cols // TILE
    place = np.arange(cols)
    source = TILE * (place % tiles) + place // tiles
    gather = np.zeros((3, cols, cols), np.float32)
    scatter = np.zeros((3, cols, cols), np.float32)
    for tap_col in range(3):
        for spot in range(cols):
            taken = source[spot] + tap_col - 1
            if 0 <= taken < cols:
                gather[tap_col, taken, spot] = 1.0
                scatter[tap_col, spot, taken] = 1.0
    return gather, scatter.reshape(3 * cols, cols)


def start_blocks(feat_hbm, feat_ref, sems):
    copies = []
    for block in range(feat_hbm.shape[1] // WIDE):
        span = slice(block * WIDE, (block + 1) * WIDE)
        copies.append(
            pltpu.make_async_copy(
                feat_hbm.at[:, span, :], feat_ref.at[:, span, :], sems.at[block]
            )
        )
        copies[-1].start()
    return copies


def pair_of(feat_ref, block):
    channels, _, cols = feat_ref.shape
    parts = [
        feat_ref[:, low : low + BLOCK, :].reshape(channels * BLOCK, cols)
        for low in range(block * WIDE, (block + 1) * WIDE, BLOCK)
    ]
    return jnp.concatenate(parts, axis=1)


def one_hot(hit):
    return jnp.where(hit, 1.0, 0.0).astype(BF16)


def banded(wout_ref, channels, lat):
    group, deep = (BLOCK + 2) * lat, channels * BLOCK
    tall = 3 * group
    place = lax.broadcasted_iota(jnp.int32, (tall, 1), 0)
    tap_col = (place >= group).astype(jnp.int32) + (place >= 2 * group).astype(jnp.int32)
    place = place - group * tap_col
    out_row = lax.div(place, jnp.full_like(place, lat))
    first = lat * tap_col + (place - lat * out_row)
    spot = lax.broadcasted_iota(jnp.int32, (1, deep), 1)
    chan = lax.div(spot, jnp.full_like(spot, BLOCK))
    gap = (spot - BLOCK * chan) - out_row
    spread = one_hot(lax.broadcasted_iota(jnp.int32, (channels, deep), 0) == chan)
    pick = lax.broadcasted_iota(jnp.int32, (tall, 9 * lat), 1)
    band = jnp.zeros((tall, deep), F32)
    for tap_row in range(3):
        taps = dot(one_hot(pick == first + 3 * lat * tap_row), wout_ref[...], 1, 0).astype(BF16)
        band = jnp.where(gap == tap_row - 2, dot(taps, spread, 1, 0), band)
    return band.astype(BF16)


def eps_kernel(step_ref, me_ref, wout_ref, noisy_ref, table_ref, feat_hbm, *refs, parts, rows, lat):
    outs = refs[:parts]
    band_ref, feat_ref, acc_ref, sum_ref, own_ref, sems = refs[parts:]
    channels, height, cols = feat_ref.shape
    copies = start_blocks(feat_hbm, feat_ref, sems)
    group = (BLOCK + 2) * lat
    band = banded(wout_ref, channels, lat)
    band_ref[...] = band
    acc_ref[...] = jnp.zeros(acc_ref.shape, F32)
    _, root_b = roots(table_ref, step_ref[0])
    edge = HALO * lat
    sum_ref[0:edge, :] = jnp.zeros((edge, cols), F32)
    sum_ref[edge + height * lat :, :] = jnp.zeros((edge, cols), F32)
    for chan in range(lat):
        own_ref[pl.ds(chan, rows, stride=lat), :] = noisy_ref[0, chan]
    for pair, copy in enumerate(copies):
        copy.wait()
        part = dot(band, pair_of(feat_ref, pair), 1, 0)
        for half in range(WIDE // BLOCK):
            low = (pair * WIDE + half * BLOCK) * lat
            span = slice(half * cols, (half + 1) * cols)
            for tap_col in range(3):
                acc_ref[tap_col, low : low + group, :] += part[
                    tap_col * group : (tap_col + 1) * group, span
                ]
    spot = lax.broadcasted_iota(jnp.int32, (height * lat, cols), 1)
    inner = slice(lat, lat + height * lat)
    left = jnp.where(spot == 0, 0.0, pltpu.roll(acc_ref[0, inner, :], 1, 1))
    right = jnp.where(spot == cols - 1, 0.0, pltpu.roll(acc_ref[2, inner, :], cols - 1, 1))
    eps = left + acc_ref[1, inner, :] + right
    sum_ref[edge : edge + height * lat, :] = -root_b * eps
    me = me_ref[0]
    low = pl.multiple_of(me * (rows * lat) + edge, 16)
    sum_ref[pl.ds(low, rows * lat), :] += own_ref[...]
    for part in range(parts):
        low = pl.multiple_of((me ^ part) * (rows * lat), 16)
        outs[part][...] = sum_ref[pl.ds(low, (rows + 2 * HALO) * lat), :].astype(BF16)


def prep_kernel(band_ref, wmid_hbm, planes_ref, wmid_ref, band_back_ref, sems):
    chans = wmid_ref.shape[1]
    copies = []
    for tap in range(9):
        copies.append(pltpu.make_async_copy(wmid_hbm.at[tap], wmid_ref.at[tap], sems.at[tap]))
        copies[-1].start()
    band_back_ref[...] = band_ref[...].T
    for tap_row in range(3):
        for tap in range(3 * tap_row, 3 * tap_row + 3):
            copies[tap].wait()
        for low in range(0, chans, PREP_ROWS):
            span = slice(low, low + PREP_ROWS)
            first = wmid_ref[3 * tap_row, span].astype(F32)
            mid = wmid_ref[3 * tap_row + 1, span].astype(F32)
            last = wmid_ref[3 * tap_row + 2, span].astype(F32)
            even = (-2.0 / 3.0) * first + (-1.0 / 3.0) * last
            odd = (-2.0 / 3.0 * PT_A) * mid
            planes_ref[0, tap_row, span] = (even + odd).astype(BF16)
            planes_ref[1, tap_row, span] = (even - odd).astype(BF16)
            even = (1.0 / 6.0) * first + (1.0 / 3.0) * last
            odd = (1.0 / 6.0 * PT_B) * mid
            planes_ref[2, tap_row, span] = (even + odd).astype(BF16)
            planes_ref[3, tap_row, span] = (even - odd).astype(BF16)


def to_planes(cells):
    tiles, chans = cells[0].shape
    none = jnp.zeros((1, chans), F32)
    d0 = jnp.concatenate([none, cells[3][: tiles - 1]], axis=0)
    d1, d2, d3, d4 = cells
    d5 = jnp.concatenate([cells[0][1:], none], axis=0)
    s1, s3 = PT_A * d1, PT_A * d3
    even_a, odd_a = d4 - 2.0 * d2, s3 - 2.0 * s1
    even_b, odd_b = d4 - 0.5 * d2, 2.0 * s3 - s1
    return (
        (d0 + d4) - 2.5 * d2,
        even_a + odd_a,
        even_a - odd_a,
        even_b + odd_b,
        even_b - odd_b,
        (d1 + d5) - 2.5 * d3,
    )


def half_from_planes(m0, ap, an, bp, bn, m5):
    sum_a, dif_a = ap + an, (0.5 * PT_A) * (ap - an)
    sum_b, dif_b = bp + bn, (0.5 * PT_B) * (bp - bn)
    return (
        0.5 * (m0 + sum_a + sum_b),
        dif_a + dif_b,
        0.25 * sum_a + sum_b,
        0.5 * dif_a + 2.0 * dif_b + 0.5 * m5,
    )


def from_planes_back(m0, ap, an, bp, bn, m5):
    sum_a, dif_a, sum_b, dif_b = ap + an, PT_A * (ap - an), bp + bn, PT_B * (bp - bn)
    return (
        m0 - 2.0 * sum_a - 0.5 * sum_b,
        -(2.0 * dif_a + 0.5 * dif_b),
        -(sum_a + sum_b),
        m5 - (dif_a + dif_b),
    )


def chunks_of(rows):
    return [(low, min(low + CHUNK, rows)) for low in range(0, rows, CHUNK)]


def decoder_kernel(step_ref, me_ref, *refs, parts, rows, lat, cols):
    blocks = refs[:parts]
    (table_ref, gather_ref, scatter_ref, taps_ref, bin_ref, bmid_ref, head_ref,
     wmid_ref, planes_ref, out_ref, lat_ref, slope_ref, high_ref, rest_ref, q_ref, lg_ref,
     tapf_ref, win_ref, *bufs) = refs[parts:]
    tiles = cols // TILE
    chans = wmid_ref.shape[1]
    hidden_rows, mixed_rows, grad_rows = rows + 6, rows + 4, rows + 2
    mixed_chunks, grad_chunks = chunks_of(mixed_rows), chunks_of(grad_rows)
    v1_refs, bufs = bufs[: len(mixed_chunks)], bufs[len(mixed_chunks) :]
    v2_refs, bufs = bufs[: len(grad_chunks)], bufs[len(grad_chunks) :]
    hg_refs, m_refs = bufs[: len(grad_chunks)], bufs[len(grad_chunks) :]

    tapf_ref[...] = jnp.zeros(tapf_ref.shape, F32)
    for tap_row in range(3):
        for tap_col in range(3):
            low = 16 * tap_col + lat * tap_row
            tapf_ref[low : low + lat, :] = taps_ref[3 * tap_row + tap_col].astype(F32)
    win_ref[...] = (0.5 * tapf_ref[...]).astype(BF16)

    me = me_ref[0]
    inside_top = jnp.where(me == 0, 0.0, 1.0).astype(F32)
    inside_bottom = jnp.where(me == parts - 1, 0.0, 1.0).astype(F32)
    root_a, root_b = roots(table_ref, step_ref[0])
    total = blocks[0][...].astype(F32)
    for block in blocks[1:]:
        total = total + block[...].astype(F32)
    latent = (total / root_a).astype(BF16)
    lat_rows = (rows + 2 * HALO) * lat
    for tap_col in range(3):
        lat_ref[tap_col, 0:lat_rows, :] = dot(latent, gather_ref[tap_col], 1, 0)
        lat_ref[tap_col, lat_rows:, :] = jnp.zeros((8, cols), F32)

    def edge(row, margin, total_rows, value):
        if row < margin:
            return value * inside_top
        if row >= total_rows - margin:
            return value * inside_bottom
        return value

    def spans(low, step=None):
        step = step or LANES
        return slice(low, min(low + step, chans))

    def put_planes(cells, row, chunks, targets, lanes):
        for plane, value in enumerate(to_planes(cells)):
            value = value.astype(BF16)
            for (low, high), target in zip(chunks, targets):
                if low <= row < high + 2:
                    target[plane, (row - low) * tiles : (row - low + 1) * tiles, lanes] = value

    def hidden_matmul(buf, plane, rows_in):
        def run():
            windows = [
                jnp.concatenate(
                    [lat_ref[tap_col, lat * row : lat * row + 16, :] for tap_col in range(3)], axis=0
                )
                for row in rows_in
            ]
            windows = jnp.concatenate(windows, axis=1).astype(BF16)
            buf[plane, 0 : len(rows_in) * cols, :] = dot(windows, win_ref[...], 0, 0)

        return run

    def hidden_piece(buf, plane, spot, row, lanes):
        def run():
            half = buf[plane, spot * cols : (spot + 1) * cols, lanes] + 0.5 * bin_ref[:, lanes]
            tanh = jnp.tanh(half)
            twice = 1.0 + tanh
            act = half * twice
            if 2 <= row < 2 + grad_rows:
                slope_ref[(row - 2) * cols : (row - 1) * cols, lanes] = (
                    twice + act * (1.0 - tanh)
                ).astype(BF16)
            act = edge(row, 3, hidden_rows, act)
            cells = [act[part * tiles : (part + 1) * tiles] for part in range(TILE)]
            put_planes(cells, row, mixed_chunks, v1_refs, lanes)

        return run

    def mixed_piece(buf, row, base, lanes):
        def run():
            span = slice((row - base) * tiles, (row - base + 1) * tiles)
            cells = half_from_planes(*[buf[plane, span, lanes] for plane in range(6)])
            grads = []
            for cell in cells:
                half = cell + 0.5 * bmid_ref[:, lanes]
                tanh = jnp.tanh(half)
                twice = 1.0 + tanh
                grad = (0.5 * head_ref[:, lanes]) * (twice + half * twice * (1.0 - tanh))
                grads.append(edge(row, 2, mixed_rows, grad))
            put_planes(grads, row, grad_chunks, v2_refs, lanes)

        return run

    def grad_piece(buf, row, base, target, lanes):
        def run():
            span = slice((row - base) * tiles, (row - base + 1) * tiles)
            cells = from_planes_back(*[buf[plane, span, lanes] for plane in range(6)])
            for part, cell in enumerate(cells):
                low = row * cols + part * tiles
                value = edge(row, 1, grad_rows, cell * slope_ref[low : low + tiles, lanes].astype(F32))
                low = (row - base) * cols + part * tiles
                target[low : low + tiles, lanes] = value.astype(BF16)

        return run

    def back_piece(low, high, target):
        def run():
            taps = dot(win_ref[...], target[...], 1, 1)
            upper = taps.astype(BF16)
            lower = (taps - upper.astype(F32)).astype(BF16)
            for row in range(low, high):
                place = slice((row - low) * cols, (row - low + 1) * cols)
                for tap_col in range(3):
                    taken = slice(16 * tap_col, 16 * tap_col + 16)
                    span = slice(tap_col * cols, (tap_col + 1) * cols)
                    high_ref[16 * row : 16 * row + 16, span] = upper[taken, place]
                    rest_ref[16 * row : 16 * row + 16, span] = lower[taken, place]

        return run

    lane_parts = [spans(low) for low in range(0, chans, LANES)]
    queue = []
    done, each = 0, CHUNK * tiles // cols
    for number, (_, high) in enumerate(mixed_chunks):
        buf, reach = m_refs[(number + 1) % len(m_refs)], min(high + 2, hidden_rows)
        groups = [range(low, min(low + each, reach)) for low in range(done, reach, each)]
        for plane, group in enumerate(groups):
            queue.append((("hidden", group[0]), -1, hidden_matmul(buf, plane, group)))
        for plane, group in enumerate(groups):
            for spot, row in enumerate(group):
                queue += [
                    (("hidden", row), -1, hidden_piece(buf, plane, spot, row, lanes))
                    for lanes in lane_parts
                ]
        done = reach
    for number, (low, high) in enumerate(mixed_chunks):
        buf = m_refs[number % len(m_refs)]
        for row in range(low, high):
            queue += [
                (("mixed", row), number, mixed_piece(buf, row, low, lanes)) for lanes in lane_parts
            ]
    for index, (low, high) in enumerate(grad_chunks):
        number = len(mixed_chunks) + index
        buf, target = m_refs[number % len(m_refs)], hg_refs[index]
        for row in range(low, high):
            queue += [
                (("grad", row), number, grad_piece(buf, row, low, target, lanes))
                for lanes in lane_parts
            ]
        queue.append((("back", low), number, back_piece(low, high, target)))
    queue.reverse()

    def flush(needed):
        while any(needed(item) for item in queue):
            queue.pop()[2]()

    def conv(step, chunk, source, back):
        low, high = chunk
        count = (high - low) * tiles
        buf = m_refs[step % len(m_refs)]
        for plane in (0, 5, 1, 2, 3, 4):
            kerns = []
            for shift in range(3):
                tap_row = 2 - shift if back else shift
                if plane in (0, 5):
                    first = (plane == 0) != back
                    kerns.append(wmid_ref[3 * tap_row + (0 if first else 2)])
                else:
                    which = (plane - 1) ^ 2 if back else plane - 1
                    kerns.append(planes_ref[which, tap_row])
            lhs = jnp.concatenate(
                [source[plane, shift * tiles : shift * tiles + count, :] for shift in range(3)], axis=1
            )
            buf[plane, 0:count, :] = dot(
                lhs, jnp.concatenate(kerns, axis=0 if back else 1), 1, 0 if back else 1
            )
            budget = QUOTA
            while budget > 0 and queue and queue[-1][1] < step:
                budget -= {"hidden": 1.0, "mixed": 1.0, "grad": 0.5, "back": 0.5}[queue[-1][0][0]]
                queue.pop()[2]()

    step = 0
    for chunk, source in zip(mixed_chunks, v1_refs):
        reach = chunk[1] + 2
        flush(lambda item: item[0][0] == "hidden" and item[0][1] < reach)
        flush(lambda item: 0 <= item[1] <= step - len(m_refs))
        conv(step, chunk, source, False)
        step += 1
    for chunk, source in zip(grad_chunks, v2_refs):
        reach = chunk[1] + 2
        flush(lambda item: item[0][0] == "mixed" and item[0][1] < reach)
        flush(lambda item: 0 <= item[1] <= step - len(m_refs))
        conv(step, chunk, source, True)
        step += 1
    flush(lambda item: True)

    q_ref[...] = dot(high_ref[...], scatter_ref[...], 1, 0) + dot(
        rest_ref[...], scatter_ref[...], 1, 0
    )
    for row in range(rows):
        lg_ref[lat * row : lat * row + lat, :] = (
            q_ref[16 * (row + 2) : 16 * (row + 2) + lat, :]
            + q_ref[16 * (row + 1) + lat : 16 * (row + 1) + 2 * lat, :]
            + q_ref[16 * row + 2 * lat : 16 * row + 3 * lat, :]
        )
    out_ref[...] = (-(root_b / root_a) * lg_ref[...]).astype(BF16)


def fill_windows(noise_ref, win_ref, lat):
    tall, cols = noise_ref.shape
    noise = noise_ref[...].astype(F32)
    spot = lax.broadcasted_iota(jnp.int32, (tall, cols), 1)
    none = jnp.zeros((lat, cols), F32)
    moved = (
        jnp.where(spot == cols - 1, 0.0, pltpu.roll(noise, cols - 1, 1)),
        noise,
        jnp.where(spot == 0, 0.0, pltpu.roll(noise, 1, 1)),
    )
    for tap_col in range(3):
        win_ref[tap_col, 0:lat, :] = none
        win_ref[tap_col, lat : lat + tall, :] = moved[tap_col]
        win_ref[tap_col, lat + tall :, :] = none


def window_of(win_ref, block, lat):
    group = (BLOCK + 2) * lat
    parts = []
    for low in range(block * WIDE * lat, (block + 1) * WIDE * lat, BLOCK * lat):
        parts.append(
            jnp.concatenate(
                [win_ref[tap_col, low : low + group, :] for tap_col in range(3)], axis=0
            )
        )
    return jnp.concatenate(parts, axis=1).astype(BF16)


def weight_kernel(
    noise_ref, thirds_ref, collect_ref, out_row_ref, in_row_ref, feat_ref, out_ref, win_ref, *, lat
):
    channels, height, _ = feat_ref.shape
    fill_windows(noise_ref, win_ref, lat)
    pairs = range(height // WIDE)
    feats = jnp.concatenate([pair_of(feat_ref, pair) for pair in pairs], axis=1)
    windows = jnp.concatenate([window_of(win_ref, pair, lat) for pair in pairs], axis=1)
    total = dot(feats, windows, 1, 1)
    gap = in_row_ref[...] - out_row_ref[...]
    kept = jnp.where((gap >= -2) & (gap <= 0), total, 0.0).astype(BF16)
    thirds = dot(thirds_ref[...], kept, 1, 0).astype(BF16)
    result = jnp.zeros(out_ref.shape, F32)
    for third in range(3):
        piece = thirds[third * channels : (third + 1) * channels]
        result = result + dot(collect_ref[third], piece, 1, 1)
    out_ref[...] = result


def feature_kernel(band_ref, noise_ref, *refs, first, lat):
    out_ref, win_ref = refs[-2:]
    channels, _, cols = out_ref.shape
    pair = pl.program_id(0) + first

    @pl.when(pl.program_id(0) == 0)
    def _():
        fill_windows(noise_ref, win_ref, lat)

    group = (BLOCK + 2) * lat
    parts = []
    for half in range(WIDE // BLOCK):
        low = pl.multiple_of((pair * WIDE + half * BLOCK) * lat, 8)
        parts.append(
            jnp.concatenate([win_ref[tap_col, pl.ds(low, group), :] for tap_col in range(3)], axis=0)
        )
    value = dot(band_ref[...], jnp.concatenate(parts, axis=1).astype(BF16), 1, 0).astype(BF16)
    for half in range(WIDE // BLOCK):
        out_ref[:, half * BLOCK : (half + 1) * BLOCK, :] = value[
            :, half * cols : (half + 1) * cols
        ].reshape(channels, BLOCK, cols)


VMEM = pl.BlockSpec(memory_space=pltpu.VMEM)
SMEM = pl.BlockSpec(memory_space=pltpu.SMEM)
ROOM = 2**20


def pinned(array):
    return pltpu.with_memory_space_constraint(jnp.asarray(array), pltpu.VMEM)


def from_hbm(array):
    return pltpu.with_memory_space_constraint(jnp.asarray(array), pltpu.HBM)


def call(kernel, scalars, operands, outs, scratch, name, left=(), room=24):
    return pl.pallas_call(
        kernel,
        in_specs=[SMEM] * len(scalars)
        + [VMEM] * len(operands)
        + [pl.BlockSpec(memory_space=pltpu.HBM)] * len(left),
        out_specs=jax.tree.map(lambda _: VMEM, outs),
        out_shape=outs,
        scratch_shapes=scratch,
        compiler_params=pltpu.CompilerParams(vmem_limit_bytes=room * ROOM),
        name=name,
    )(*scalars, *operands, *(from_hbm(one) for one in left))


def eps_call(step, me, feats, kern, noisy, parts, rows):
    channels, height, cols = feats.shape
    lat = noisy.shape[1]
    block_rows = (rows + 2 * HALO) * lat
    *blocks, band = call(
        functools.partial(eps_kernel, parts=parts, rows=rows, lat=lat),
        (step, me),
        (from_hbm(kern), from_hbm(noisy), from_hbm(schedule_table())),
        [pltpu.VMEM((block_rows, cols), BF16) for _ in range(parts)]
        + [pltpu.VMEM((3 * (BLOCK + 2) * lat, channels * BLOCK), BF16)],
        [
            pltpu.VMEM((channels, height, cols), BF16),
            pltpu.VMEM((3, (height + 2) * lat, cols), F32),
            pltpu.VMEM(((height + 2 * HALO) * lat, cols), F32),
            pltpu.VMEM((rows * lat, cols), F32),
            pltpu.SemaphoreType.DMA((height // WIDE,)),
        ],
        "eps_partial",
        (feats,),
    )
    return blocks, band


def prep_call(w_mid, band):
    chans = w_mid.shape[1]
    return call(
        prep_kernel,
        (),
        (pinned(band),),
        [pltpu.VMEM((4, 3, chans, chans), BF16), pltpu.VMEM(w_mid.shape, BF16),
         pltpu.VMEM(band.shape[::-1], BF16)],
        [pltpu.SemaphoreType.DMA((9,))],
        "weight_planes",
        (w_mid,),
    )


def decoder_call(step, me, moved, taps, b_in, b_mid, head, w_mid, planes, rows):
    lat, chans = taps.shape[1:]
    block_rows, cols = moved[0].shape
    tiles = cols // TILE
    gather, scatter = (jnp.asarray(part, BF16) for part in column_tables(cols))
    mixed_chunks, grad_chunks = chunks_of(rows + 4), chunks_of(rows + 2)
    tall_rows = [(high - low + 2) * tiles for low, high in mixed_chunks]
    back_rows = [(high - low + 2) * tiles for low, high in grad_chunks]
    return call(
        functools.partial(decoder_kernel, parts=len(moved), rows=rows, lat=lat, cols=cols),
        (step, me),
        tuple(pinned(one) for one in (
            *moved, schedule_table(), gather, scatter, taps, b_in[None, :], b_mid[None, :],
            head[None, :], w_mid, planes,
        )),
        jax.ShapeDtypeStruct((rows * lat, cols), BF16),
        [
            pltpu.VMEM((3, block_rows + 8, cols), F32),
            pltpu.VMEM(((rows + 2) * cols, chans), BF16),
            pltpu.VMEM(((rows + 2) * 16, 3 * cols), BF16),
            pltpu.VMEM(((rows + 2) * 16, 3 * cols), BF16),
            pltpu.VMEM(((rows + 2) * 16, cols), F32),
            pltpu.VMEM((rows * lat, cols), F32),
            pltpu.VMEM((48, chans), F32),
            pltpu.VMEM((48, chans), BF16),
        ]
        + [pltpu.VMEM((6, size, chans), BF16) for size in tall_rows + back_rows]
        + [pltpu.VMEM(((high - low) * cols, chans), BF16) for low, high in grad_chunks]
        + [pltpu.VMEM((6, CHUNK * tiles, chans), F32) for _ in range(3)],
        "decoder",
        room=46,
    )


def weight_call(feats, full, tables, lat):
    channels, height, cols = feats.shape
    return call(
        functools.partial(weight_kernel, lat=lat),
        (),
        (full, pinned(tables["thirds"]), pinned(tables["collect"]),
         pinned(tables["out_row"][None, :]), pinned(tables["in_row"][:, None]), pinned(feats)),
        jax.ShapeDtypeStruct((9 * lat, channels), F32),
        [pltpu.VMEM((3, (height + 2) * lat, cols), F32)],
        "weight_grad",
    )


def feature_call(band, full, channels, height, lat, first, last, before=None):
    cols = full.shape[1]
    extra = [] if before is None else [before]
    return pl.pallas_call(
        functools.partial(feature_kernel, first=first, lat=lat),
        grid=(last - first,),
        in_specs=[pl.BlockSpec(one.shape, lambda pair: (0, 0)) for one in (band, full)]
        + [pl.BlockSpec(memory_space=pltpu.HBM) for _ in extra],
        out_specs=pl.BlockSpec((channels, WIDE, cols), lambda pair: (0, pair + first, 0)),
        out_shape=jax.ShapeDtypeStruct((channels, height, cols), BF16),
        scratch_shapes=[pltpu.VMEM((3, (height + 2) * lat, cols), F32)],
        input_output_aliases={2: 0} if extra else {},
        compiler_params=pltpu.CompilerParams(vmem_limit_bytes=24 * ROOM),
        name="feature_grads",
    )(pinned(band), full, *extra)


def tables_of(channels, lat):
    names = ("out_row", "in_row", "thirds", "collect")
    tables = dict(zip(names, band_tables(channels, lat)))
    return {
        name: value if value.dtype == np.int32 else jnp.asarray(value, BF16)
        for name, value in tables.items()
    }


def body(features, w_out, noisy_latent, timestep, w_in, b_in, w_mid, b_mid, reward_head):
    _, channels, height, cols = features.shape
    lat, rows = noisy_latent.shape[1:3]
    parts, images = lax.axis_size("mp"), lax.axis_size("dp")
    feats, kern = features[0], w_out.T
    me = lax.axis_index("mp").astype(jnp.int32).reshape(1)
    tables = tables_of(channels, lat)
    blocks, band = eps_call(timestep, me, feats, kern, noisy_latent, parts, rows)
    moved = [blocks[0]] + [
        lax.ppermute(blocks[part], "mp", [(i, i ^ part) for i in range(parts)])
        for part in range(1, parts)
    ]
    planes, w_mid, band = prep_call(w_mid, band)
    taps = jnp.transpose(w_in, (0, 2, 1))
    noise = decoder_call(
        timestep, me, moved, taps, b_in, b_mid, reward_head, w_mid, planes, rows
    )
    full = lax.all_gather(noise, "mp", axis=0, tiled=True)
    weight_grad = weight_call(feats, full, tables, lat)
    pairs = height // WIDE
    stage, feature_grads = 1, None
    while stage < images:
        other = lax.ppermute(weight_grad, "dp", [(i, i ^ stage) for i in range(images)])
        if stage == 1:
            feature_grads = feature_call(band, full, channels, height, lat, 0, pairs // 2)
            other, feature_grads = lax.optimization_barrier((other, feature_grads))
        weight_grad = weight_grad + other
        stage *= 2
    feature_grads = feature_call(
        band, full, channels, height, lat, pairs // 2, pairs, feature_grads
    )
    return feature_grads[None], (weight_grad / (height * cols)).T


def solution(mesh):
    in_specs = (
        P("dp", "mp", None, None),
        P("mp", None),
        P("dp", None, "mp", None),
        P("dp"),
        P(),
        P(),
        P(),
        P(),
        P(),
    )
    out_specs = (P("dp", "mp", None, None), P("mp", None))
    return jax.shard_map(body, mesh=mesh, in_specs=in_specs, out_specs=out_specs, check_vma=False)
```
